512 devices in a mesh: gal: 64 (over x, z, core), pix: 8 (over y).
Axes of the slice: x: 4, y: 8, z: 8, core: 2. Of those that a mesh axis runs over, the one named last changes fastest.
Arguments:
- spectra: bfloat16 [32768, 8192], P('gal', 'pix'), may hold values from -500 to 500
- sketch: bfloat16 [32768, 128], P('gal'), may hold values from -0.25 to 0.25
- block_mask: int32 [64, 64], P('gal', 'pix'), may hold values from 0 to 1, as said below
- rank_key: int32 [64], P('gal'), may hold values from 0 to 63, each once
Outputs:
- projector_basis: float32 [8192, 128], P('pix')
- scores: float32 [32768, 128], P('gal')
The draws below stay inside these ranges and needn't reach their ends.
Inputs may be any that keep to these rules, and one draw needn't show every extreme that they name: `block_mask`: in every galaxy batch at least half of the 64 blocks are valid.
All inputs are finite; a program needn't handle non-finite values.
Results may differ from the reference program's by a relative error of at most 0.0059.
Values sent between devices are 32-bit elements; how exact they have to be, the bound alone decides.
No kernel may reach another device: no remote copies, remote signals or barrier semaphores. Data moves between devices by JAX's collectives and lax.ppermute only.
A program may use at most 64 MiB of HBM per device.

```python
import math
import jax
import jax.numpy as jnp
from jax import lax

NPIX = 8192
K = 128
B_DEV = 512
ITERS = 2
BLOCK = 128
LEVELS = 6
SPECTRA = 32768
NBLK = 64
N_GAL = 64


def draw_spectra(key, part):
    key_pix, key_row, key_noise = jax.random.split(jax.random.fold_in(key, 11), 3)
    pixel_scale = jnp.exp(jax.random.uniform(key_pix, (1, NPIX), minval=0.0, maxval=math.log(10.0)))
    row_scale = jnp.exp(jax.random.uniform(key_row, (SPECTRA, 1), minval=0.0, maxval=math.log(10.0)))
    noise = jax.random.truncated_normal(key_noise, -4.0, 4.0, (SPECTRA, NPIX))
    values = row_scale * pixel_scale * noise
    return values.astype(jnp.float32).astype(jnp.bfloat16)


def draw_block_mask(key, part):
    key_coin, key_perm = jax.random.split(jax.random.fold_in(key, 23))
    coins = jax.random.randint(key_coin, (N_GAL, NBLK), 0, 4)
    orders = jax.vmap(lambda sub_key: jax.random.permutation(sub_key, NBLK))(jax.random.split(key_perm, N_GAL))
    forced = orders < NBLK // 2
    return jnp.where(forced | (coins > 0), 1, 0).astype(jnp.int32)


def block_levels(rng, extent, cuts, smallest, largest):
    gain, own = 1.0, jax.random.fold_in(rng, 6)
    for axis_at, blocks in cuts:
        draws = jnp.exp(jax.random.uniform(jax.random.fold_in(own, axis_at), (blocks,), jnp.float32, smallest / len(cuts), largest / len(cuts)))
        gain = gain * jnp.repeat(draws, extent[axis_at] // blocks).reshape([-1 if axis == axis_at else 1 for axis in range(len(extent))])
    return gain


def gaussian(own_key, dims, spread, limit, shards=(), kind=jnp.bfloat16):
    result = spread * jax.random.normal(own_key, dims, jnp.float32)
    if shards:
        result = result * block_levels(own_key, dims, shards, -0.22, 0.18)
    return jnp.clip(result, -limit, limit).astype(kind)


def setup_inputs(seed: int = 0) -> dict:
    seeds = jax.random.split(jax.random.key(seed), 5)
    spectra = draw_spectra(jax.random.fold_in(seeds[4], 71), 0)
    sketch = gaussian(seeds[1], (SPECTRA, K), B_DEV ** -0.5, 0.25, ((0, 64),))
    block_mask = draw_block_mask(jax.random.fold_in(seeds[4], 71), 0)
    rank_key = jax.random.permutation(seeds[3], N_GAL).astype(jnp.int32)
    return dict(spectra=spectra, sketch=sketch, block_mask=block_mask, rank_key=rank_key)


def gram_of(left_side, right_side):
    return lax.dot_general(left_side.astype(jnp.float32), right_side.astype(jnp.float32), (((0,), (0,)), ((), ())), precision=lax.Precision.HIGHEST, preferred_element_type=jnp.float32)

def matmul_high(left_side, right_side):
    return jnp.dot(left_side.astype(jnp.float32), right_side.astype(jnp.float32), precision=lax.Precision.HIGHEST, preferred_element_type=jnp.float32)

def orthonormal(columns, gram_matrix):
    lower_factor = jnp.linalg.cholesky(gram_matrix)
    return lax.linalg.triangular_solve(lower_factor, columns, left_side=False, lower=True, transpose_a=True)

def masked_batch(spectra_g, mask_g):
    pixel_mask = jnp.repeat(mask_g, BLOCK).astype(jnp.bfloat16)
    return spectra_g * pixel_mask[None, :]

def leaf_basis(shard_args):
    spectra_g, sketch_g, mask_g = shard_args
    masked = masked_batch(spectra_g, mask_g)
    sketched = lax.dot_general(masked.astype(jnp.float32), sketch_g.astype(jnp.float32), (((0,), (0,)), ((), ())), preferred_element_type=jnp.float32)
    ortho_panel = orthonormal(sketched, gram_of(sketched, sketched))
    projected = jnp.dot(masked.astype(jnp.float32), ortho_panel.astype(jnp.bfloat16).astype(jnp.float32), preferred_element_type=jnp.float32)
    factor = jnp.linalg.cholesky(gram_of(projected, projected))
    return matmul_high(ortho_panel, factor)

def merge_pair(front_panel, back_panel):
    joined = jnp.concatenate([front_panel, back_panel], axis=1)
    gram_matrix = gram_of(joined, joined)
    rotation = jnp.concatenate([jnp.eye(K, dtype=jnp.float32), jnp.zeros((K, K), jnp.float32)], axis=0)
    for iteration in range(ITERS):
        mapped = matmul_high(gram_matrix, rotation)
        rotation = orthonormal(mapped, gram_of(mapped, mapped))
    return (matmul_high(joined, rotation), gram_of(rotation, matmul_high(gram_matrix, rotation)))

def reference(spectra, sketch, block_mask, rank_key):
    batches = spectra.reshape(N_GAL, B_DEV, NPIX)
    all_bases = lax.map(leaf_basis, (batches, sketch.reshape(N_GAL, B_DEV, K), block_mask))
    group_keys = rank_key
    group_count = N_GAL
    all_grams = None
    for section in range(LEVELS):
        paired = all_bases.reshape(group_count // 2, 2, NPIX, K)
        key_pairs = group_keys.reshape(group_count // 2, 2)
        lead_flag = (key_pairs[:, 0] < key_pairs[:, 1])[:, None, None]
        front_panels = jnp.where(lead_flag, paired[:, 0], paired[:, 1])
        back_panels = jnp.where(lead_flag, paired[:, 1], paired[:, 0])
        all_bases, all_grams = lax.map(lambda both: merge_pair(both[0], both[1]), (front_panels, back_panels))
        group_keys = lax.optimization_barrier(jnp.min(key_pairs, axis=1))
        group_count = group_count // 2
    projector_basis = orthonormal(all_bases[0], all_grams[0]) * math.sqrt(NPIX)
    basis_half = projector_basis.astype(jnp.bfloat16)

    def batch_scores(shard_args):
        masked = masked_batch(shard_args[0], shard_args[1])
        return jnp.dot(masked.astype(jnp.float32), basis_half.astype(jnp.float32), preferred_element_type=jnp.float32) / NPIX
    scores = lax.map(batch_scores, (batches, block_mask)).reshape(SPECTRA, K)
    return (projector_basis, scores)
```

```python
import functools
import math

import jax
import jax.numpy as jnp
from jax import lax
from jax.experimental import pallas as pl
from jax.experimental.pallas import tpu as pltpu
from jax.sharding import PartitionSpec as P

NPIX = 8192
K = 128
PIX = 8
HIGH = lax.Precision.HIGHEST
PARAMS = pltpu.CompilerParams(vmem_limit_bytes=32 * 1024 * 1024)
NB = 32


def dot_of(a, b, dims):
    return lax.dot_general(
        a, b, (dims, ((), ())), precision=HIGH, preferred_element_type=jnp.float32
    )


def nn(a, b):
    return dot_of(a, b, ((1,), (0,)))


def nt(a, b):
    return dot_of(a, b, ((1,), (1,)))


def tn(a, b):
    return dot_of(a, b, ((0,), (0,)))


def split3(x):
    high = x.astype(jnp.bfloat16)
    rest = x - high.astype(jnp.float32)
    middle = rest.astype(jnp.bfloat16)
    low = (rest - middle.astype(jnp.float32)).astype(jnp.bfloat16)
    return high, middle, low


def tn_thin(a, b):
    ah, am, al = split3(a)
    bh, bm, bl = split3(b)
    left = jnp.concatenate([ah, ah, am, am, ah, al], axis=0)
    right = jnp.concatenate([bh, bm, bh, bm, bl, bh], axis=0)
    return lax.dot_general(
        left, right, (((0,), (0,)), ((), ())), preferred_element_type=jnp.float32
    )


def eliminate(work):
    row_id = lax.broadcasted_iota(jnp.int32, (NB, 1), 0)
    for start in range(0, K, NB):
        rows = work[start : start + NB, :]
        for step in range(NB):
            at = start + step
            pivot_row = rows[step : step + 1, :]
            inverse = lax.rsqrt(pivot_row[:, at : at + 1])
            scaled = pivot_row * inverse
            if step < NB - 1:
                column = jnp.where(row_id > step, rows[:, at : at + 1] * inverse, 0.0)
                rows = jnp.where(row_id == step, scaled, rows - column * scaled)
            else:
                rows = jnp.where(row_id == step, scaled, rows)
        work[start : start + NB, :] = rows
        if start + NB < K:
            work[start + NB :, :] = work[start + NB :, :] - tn_thin(
                rows[:, start + NB : K], rows
            )


def leaf_kernel(parts, sketched, out, work_z, work_h):
    rows = sketched.shape[0]
    work_h[...] = jnp.sum(parts[:, :K, :], axis=0)
    for part in range(PIX):
        work_z[16 * part : 16 * (part + 1), :K] = parts[part, K:, :]
    row_at = lax.broadcasted_iota(jnp.int32, (K, K), 0)
    col_at = lax.broadcasted_iota(jnp.int32, (K, K), 1)
    work_z[:, K:] = jnp.where(row_at == col_at, 1.0, 0.0)
    eliminate(work_z)
    eliminate(work_h)
    inverse = work_z[:, K:]
    factor = nt(inverse, jnp.where(col_at >= row_at, work_h[...], 0.0))
    out[:rows, :] = nn(sketched[...], tn(inverse, factor))
    out[rows : rows + K, :] = tn(factor, factor)


def merge_kernel(last, parts, front, back, out, gram, work):
    rows = front.shape[0] - K - 8
    cross = jnp.sum(parts[...], axis=0)
    front_gram = front[rows : rows + K, :]
    back_gram = back[rows : rows + K, :]
    largest = jnp.maximum(
        jnp.max(front_gram, keepdims=True), jnp.max(back_gram, keepdims=True)
    )
    scale = 1.0 / largest
    gram[:K, :K] = front_gram * scale
    gram[:K, K:] = cross * scale
    gram[K:, :K] = cross.T * scale
    gram[K:, K:] = back_gram * scale
    powered = nn(gram[:K, :], gram[...])
    if last:
        work[:, :K] = nt(nn(powered, gram[...]), powered)
    else:
        work[:, :K] = nt(powered, powered)
    work[:, K:] = powered
    eliminate(work)
    rotation = work[:, K:]
    panel = nt(front[:rows, :], rotation[:, :K]) + nt(back[:rows, :], rotation[:, K:])
    if last:
        out[...] = panel * (math.sqrt(NPIX) * jnp.sqrt(scale))
    else:
        out[:rows, :] = panel
        out[rows : rows + K, :] = nt(nn(rotation, gram[...]), rotation) * largest
        out[rows + K :, :] = jnp.minimum(front[rows + K :, :], back[rows + K :, :])


def swapped(block, axis, bit):
    count = lax.axis_size(axis)
    return lax.ppermute(block, axis, [(low, low ^ 1 << bit) for low in range(count)])


def spread(block):
    many = jnp.broadcast_to(block[None], (PIX,) + block.shape)
    return lax.all_to_all(many, "pix", 0, 0)


def per_device(spectra, sketch, block_mask, rank_key):
    batch, width = spectra.shape
    share = batch // PIX
    pixel_mask = jnp.repeat(block_mask[0], width // block_mask.shape[1]).astype(jnp.bfloat16)
    masked = spectra * pixel_mask[None, :]
    sketched = lax.dot_general(
        masked, sketch, (((0,), (0,)), ((), ())), preferred_element_type=jnp.float32
    )
    sketch_gram = tn(sketched, sketched)
    high = sketched.astype(jnp.bfloat16)
    low = (sketched - high.astype(jnp.float32)).astype(jnp.bfloat16)
    both = jnp.dot(
        masked, jnp.concatenate([high, low], axis=1), preferred_element_type=jnp.float32
    )
    projected = both[:, :K] + both[:, K:]
    sends = jnp.concatenate(
        [projected.reshape(PIX, share, K), sketch_gram.reshape(PIX, K // PIX, K)], axis=1
    )
    summed = jnp.sum(lax.all_to_all(sends, "pix", 0, 0), axis=0)
    own_rows = summed[:share]
    parts = spread(jnp.concatenate([tn(own_rows, own_rows), summed[share:]], axis=0))
    state = pl.pallas_call(
        leaf_kernel,
        out_shape=jax.ShapeDtypeStruct((width + K, K), jnp.float32),
        scratch_shapes=[pltpu.VMEM((K, 2 * K), jnp.float32), pltpu.VMEM((K, K), jnp.float32)],
        compiler_params=PARAMS,
        name="leaf",
    )(parts, sketched)
    key_rows = jnp.broadcast_to(rank_key.astype(jnp.float32)[:, None], (8, K))
    state = jnp.concatenate([state, key_rows], axis=0)
    level_count = lax.axis_size("gal").bit_length() - 1
    for level in range(level_count):
        last = level == level_count - 1
        partner = swapped(state, "gal", level)
        lead_flag = state[width + K, 0] < partner[width + K, 0]
        front = jnp.where(lead_flag, state, partner)
        back = jnp.where(lead_flag, partner, state)
        parts = spread(tn(front[:width], back[:width]))
        out_rows = width if last else width + K + 8
        state = pl.pallas_call(
            functools.partial(merge_kernel, last),
            out_shape=jax.ShapeDtypeStruct((out_rows, K), jnp.float32),
            scratch_shapes=[
                pltpu.VMEM((2 * K, 2 * K), jnp.float32),
                pltpu.VMEM((K, 3 * K), jnp.float32),
            ],
            compiler_params=PARAMS,
            name="finish" if last else "merge",
        )(parts, front, back)
    basis_half = state.astype(jnp.bfloat16)
    score_terms = jnp.dot(masked, basis_half, preferred_element_type=jnp.float32)
    own_scores = jnp.sum(
        lax.all_to_all(score_terms.reshape(PIX, share, K), "pix", 0, 0), axis=0
    )
    scores = spread(own_scores * (1.0 / NPIX)).reshape(batch, K)
    return (state, scores)


def solution(mesh):
    in_specs = (P("gal", "pix"), P("gal", None), P("gal", "pix"), P("gal"))
    out_specs = (P("pix", None), P("gal", None))
    return jax.shard_map(
        per_device, mesh=mesh, in_specs=in_specs, out_specs=out_specs, check_vma=False
    )
```

```python
import functools
import math

import jax
import jax.numpy as jnp
from jax import lax
from jax.experimental import pallas as pl
from jax.experimental.pallas import tpu as pltpu
from jax.sharding import PartitionSpec as P

NPIX = 8192
K = 128
PIX = 8
HIGH = lax.Precision.HIGHEST
PARAMS = pltpu.CompilerParams(vmem_limit_bytes=32 * 1024 * 1024)
NB = 32
LANES = 128


def dot_of(a, b, dims):
    return lax.dot_general(
        a, b, (dims, ((), ())), precision=HIGH, preferred_element_type=jnp.float32
    )


def nn(a, b):
    return dot_of(a, b, ((1,), (0,)))


def nt(a, b):
    return dot_of(a, b, ((1,), (1,)))


def tn(a, b):
    return dot_of(a, b, ((0,), (0,)))


def split3(x):
    high = x.astype(jnp.bfloat16)
    rest = x - high.astype(jnp.float32)
    middle = rest.astype(jnp.bfloat16)
    low = (rest - middle.astype(jnp.float32)).astype(jnp.bfloat16)
    return high, middle, low


def tn_thin(a, b):
    ah, am, al = split3(a)
    bh, bm, bl = split3(b)
    left = jnp.concatenate([ah, ah, am, am, ah, al], axis=0)
    right = jnp.concatenate([bh, bm, bh, bm, bl, bh], axis=0)
    return lax.dot_general(
        left, right, (((0,), (0,)), ((), ())), preferred_element_type=jnp.float32
    )


def whole(x):
    return jnp.broadcast_to(x, (8, LANES))


def across(x, width):
    return jnp.concatenate([x] * (width // LANES), axis=1)


def eliminate_rows(work, at):
    width = work.shape[1]
    end = (at // NB + 1) * NB
    count = (end - at) // 8 - 1
    sub = lax.broadcasted_iota(jnp.int32, (8, width), 0)
    pivots = [jnp.broadcast_to(work[at + i : at + i + 1, :K], (8, K)) for i in range(8)]
    block = [[whole(pivots[i][:, at + k : at + k + 1]) for k in range(i + 1)] for i in range(8)]
    columns = None
    if count:
        columns = [
            jnp.broadcast_to(work[at + 8 : end, at + k : at + k + 1], (8 * count, LANES)).reshape(
                count, 8, LANES
            )
            for k in range(8)
        ]
    lower, scaled_rows, multipliers = [], [], []
    result = None
    for j in range(8):
        inverse = lax.rsqrt(block[j][j])
        factors = [block[i][j] * inverse if i > j else None for i in range(8)]
        for k in range(j + 1, 8):
            for i in range(k, 8):
                block[i][k] = block[i][k] - factors[i] * factors[k]
        if count:
            multiplier = columns[j] * inverse[None]
            for k in range(j + 1, 8):
                columns[k] = columns[k] - multiplier * factors[k][None]
            multipliers.append(multiplier)
        row = jnp.broadcast_to(work[at + j : at + j + 1, :], (8, width))
        for q in range(j):
            row = row - across(lower[q][j], width) * scaled_rows[q]
        row = row * across(inverse, width)
        lower.append(factors)
        scaled_rows.append(row)
        result = row if result is None else jnp.where(sub >= j, row, result)
    work[at : at + 8, :] = result
    for t in range(count):
        rows = work[at + 8 + 8 * t : at + 16 + 8 * t, :]
        for j in range(8):
            rows = rows - across(multipliers[j][t], width) * scaled_rows[j]
        work[at + 8 + 8 * t : at + 16 + 8 * t, :] = rows
    if at + 8 == end and end < K:
        group = work[end - NB : end, :]
        work[end:, :] = work[end:, :] - tn_thin(group[:, end:K], group)


def eliminate(*works):
    for at in range(0, K, 8):
        for work in works:
            eliminate_rows(work, at)


def leaf_kernel(parts, sketched, panel, gram, work_z, work_h):
    work_h[...] = jnp.sum(parts[:, :K, :], axis=0)
    for part in range(PIX):
        work_z[16 * part : 16 * (part + 1), :K] = parts[part, K:, :]
    row_at = lax.broadcasted_iota(jnp.int32, (K, K), 0)
    col_at = lax.broadcasted_iota(jnp.int32, (K, K), 1)
    work_z[:, K:] = jnp.where(row_at == col_at, 1.0, 0.0)
    eliminate(work_z, work_h)
    inverse = work_z[:, K:]
    factor = nt(inverse, jnp.where(col_at >= row_at, work_h[...], 0.0))
    panel[...] = nn(sketched[...], tn(inverse, factor))
    gram[...] = tn(factor, factor)


def merge_kernel(last, core, keys, mine, other, own_gram, partner_gram, front, back, *refs):
    out, gram, work = refs[0], refs[-2], refs[-1]
    rows = front.shape[0]
    half = K // 2
    second = core[:1, :] > 0.5
    lead = keys[:1, :] < keys[8:9, :]
    top = jnp.where(second, other[...], mine[...])
    low = jnp.where(second, mine[...], other[...])
    front_gram = jnp.where(lead, own_gram[...], partner_gram[...])
    back_gram = jnp.where(lead, partner_gram[...], own_gram[...])
    largest = jnp.maximum(
        jnp.max(front_gram, keepdims=True), jnp.max(back_gram, keepdims=True)
    )
    scale = 1.0 / largest
    gram[:K, :K] = front_gram * scale
    gram[:half, K:] = top * scale
    gram[half:K, K:] = low * scale
    gram[K:, :K] = gram[:K, K:].T
    gram[K:, K:] = back_gram * scale
    powered = nn(gram[:K, :], gram[...])
    if last:
        work[:, :K] = nt(nn(powered, gram[...]), powered)
    else:
        work[:, :K] = nt(powered, powered)
    work[:, K:] = powered
    eliminate(work)
    rotation = work[:, K:]
    panel = nt(front[...], rotation[:, :K]) + nt(back[...], rotation[:, K:])
    if last:
        out[...] = panel * (math.sqrt(NPIX) * jnp.sqrt(scale))
    else:
        out[:rows, :] = panel
        merged = nt(nn(rotation, gram[...]), rotation) * largest
        refs[1][...] = merged
        out[rows : rows + half, :] = jnp.where(second, merged[half:, :], merged[:half, :])
        out[rows + half :, :] = jnp.minimum(keys[:8, :], keys[8:, :])


def swapped(block, axis, bit):
    count = lax.axis_size(axis)
    return lax.ppermute(block, axis, [(low, low ^ 1 << bit) for low in range(count)])


def spread(block):
    many = jnp.broadcast_to(block[None], (PIX,) + block.shape)
    return lax.all_to_all(many, "pix", 0, 0)


def per_device(spectra, sketch, block_mask, rank_key):
    batch, width = spectra.shape
    share = batch // PIX
    rows = width // 2
    half = K // 2
    second = lax.axis_index("gal") % 2 == 1
    core_rows = jnp.broadcast_to(second.astype(jnp.float32), (8, K))
    pixel_mask = jnp.repeat(block_mask[0], width // block_mask.shape[1]).astype(jnp.bfloat16)
    masked = spectra * pixel_mask[None, :]
    sketched = lax.dot_general(
        masked, sketch, (((0,), (0,)), ((), ())), preferred_element_type=jnp.float32
    )
    sketch_gram = tn(sketched, sketched)
    high = lax.reduce_precision(sketched, 8, 7)
    low = sketched - high
    pieces = jnp.concatenate([high.astype(jnp.bfloat16), low.astype(jnp.bfloat16)], axis=1)
    both = jnp.dot(masked, pieces, preferred_element_type=jnp.float32)
    projected = both[:, :K] + both[:, K:]
    sends = jnp.concatenate(
        [projected.reshape(PIX, share, K), sketch_gram.reshape(PIX, K // PIX, K)], axis=1
    )
    summed = jnp.sum(lax.all_to_all(sends, "pix", 0, 0), axis=0)
    own_rows = summed[:share]
    parts = spread(jnp.concatenate([tn(own_rows, own_rows), summed[share:]], axis=0))
    leaf_panel, own_gram = pl.pallas_call(
        leaf_kernel,
        out_shape=[
            jax.ShapeDtypeStruct((width, K), jnp.float32),
            jax.ShapeDtypeStruct((K, K), jnp.float32),
        ],
        scratch_shapes=[pltpu.VMEM((K, 2 * K), jnp.float32), pltpu.VMEM((K, K), jnp.float32)],
        compiler_params=PARAMS,
        name="leaf",
    )(parts, sketched)
    key_rows = jnp.broadcast_to(rank_key.astype(jnp.float32)[:, None], (8, K))
    kept = jnp.where(second, leaf_panel[rows:], leaf_panel[:rows])
    sent = jnp.where(second, leaf_panel[:rows], leaf_panel[rows:])
    got = swapped(jnp.concatenate([sent, own_gram, key_rows], axis=0), "gal", 0)
    other_panel, partner_gram, other_key = got[:rows], got[rows : rows + K], got[rows + K :]
    level_count = lax.axis_size("gal").bit_length() - 1
    for level in range(level_count):
        last = level == level_count - 1
        if level:
            got = swapped(state, "gal", level)
            kept, key_rows = state[:rows], state[rows + half :]
            other_panel, other_key = got[:rows], got[rows + half :]
        lead = key_rows[:1] < other_key[:1]
        front = jnp.where(lead, kept, other_panel)
        back = jnp.where(lead, other_panel, kept)
        cross = tn(front, back)
        cross_sent = jnp.where(second, cross[:half], cross[half:])
        cross_kept = jnp.where(second, cross[half:], cross[:half])
        mine = jnp.sum(spread(cross_kept + swapped(cross_sent, "gal", 0)), axis=0)
        if level:
            gram_half = got[rows : rows + half]
            other = swapped(jnp.concatenate([mine, gram_half], axis=0), "gal", 0)
            other, other_half = other[:half], other[half:]
            partner_gram = jnp.concatenate(
                [
                    jnp.where(second, other_half, gram_half),
                    jnp.where(second, gram_half, other_half),
                ],
                axis=0,
            )
        else:
            other = swapped(mine, "gal", 0)
        keys = jnp.concatenate([key_rows, other_key], axis=0)
        if last:
            out_shape = jax.ShapeDtypeStruct((rows, K), jnp.float32)
        else:
            out_shape = [
                jax.ShapeDtypeStruct((rows + half + 8, K), jnp.float32),
                jax.ShapeDtypeStruct((K, K), jnp.float32),
            ]
        state = pl.pallas_call(
            functools.partial(merge_kernel, last),
            out_shape=out_shape,
            scratch_shapes=[
                pltpu.VMEM((2 * K, 2 * K), jnp.float32),
                pltpu.VMEM((K, 3 * K), jnp.float32),
            ],
            compiler_params=PARAMS,
            name="finish" if last else "merge",
        )(core_rows, keys, mine, other, own_gram, partner_gram, front, back)
        if not last:
            state, own_gram = state
    other = swapped(state, "gal", 0)
    basis = jnp.concatenate(
        [jnp.where(second, other, state), jnp.where(second, state, other)], axis=0
    )
    score_terms = jnp.dot(masked, basis.astype(jnp.bfloat16), preferred_element_type=jnp.float32)
    own_scores = jnp.sum(
        lax.all_to_all(score_terms.reshape(PIX, share, K), "pix", 0, 0), axis=0
    )
    scores = spread(own_scores * (1.0 / NPIX)).reshape(batch, K)
    return (basis, scores)


def solution(mesh):
    in_specs = (P("gal", "pix"), P("gal", None), P("gal", "pix"), P("gal"))
    out_specs = (P("pix", None), P("gal", None))
    return jax.shard_map(
        per_device, mesh=mesh, in_specs=in_specs, out_specs=out_specs, check_vma=False
    )
```

```python
import functools
import math

import jax
import jax.numpy as jnp
from jax import lax
from jax.experimental import pallas as pl
from jax.experimental.pallas import tpu as pltpu
from jax.sharding import PartitionSpec as P

NPIX = 8192
K = 128
PIX = 8
HIGH = lax.Precision.HIGHEST
PARAMS = pltpu.CompilerParams(vmem_limit_bytes=32 * 1024 * 1024)
NB = 32
LANES = 128


def dot_of(a, b, dims):
    return lax.dot_general(
        a, b, (dims, ((), ())), precision=HIGH, preferred_element_type=jnp.float32
    )


def nn(a, b):
    return dot_of(a, b, ((1,), (0,)))


def nt(a, b):
    return dot_of(a, b, ((1,), (1,)))


def tn(a, b):
    return dot_of(a, b, ((0,), (0,)))


def split3(x):
    high = x.astype(jnp.bfloat16)
    rest = x - high.astype(jnp.float32)
    middle = rest.astype(jnp.bfloat16)
    low = (rest - middle.astype(jnp.float32)).astype(jnp.bfloat16)
    return high, middle, low


def tn_thin(a, b):
    ah, am, al = split3(a)
    bh, bm, bl = split3(b)
    left = jnp.concatenate([ah, ah, am, am, ah, al], axis=0)
    right = jnp.concatenate([bh, bm, bh, bm, bl, bh], axis=0)
    return lax.dot_general(
        left, right, (((0,), (0,)), ((), ())), preferred_element_type=jnp.float32
    )


def whole(x):
    return jnp.broadcast_to(x, (8, LANES))


def across(x, width):
    return jnp.concatenate([x] * (width // LANES), axis=1)


def eliminate_rows(work, at):
    width = work.shape[1]
    end = (at // NB + 1) * NB
    count = (end - at) // 8 - 1
    sub = lax.broadcasted_iota(jnp.int32, (8, width), 0)
    pivots = [jnp.broadcast_to(work[at + i : at + i + 1, :K], (8, K)) for i in range(8)]
    block = [[whole(pivots[i][:, at + k : at + k + 1]) for k in range(i + 1)] for i in range(8)]
    columns = None
    if count:
        columns = [
            jnp.broadcast_to(work[at + 8 : end, at + k : at + k + 1], (8 * count, LANES)).reshape(
                count, 8, LANES
            )
            for k in range(8)
        ]
    lower, scaled_rows, multipliers = [], [], []
    result = None
    for j in range(8):
        inverse = lax.rsqrt(block[j][j])
        factors = [block[i][j] * inverse if i > j else None for i in range(8)]
        for k in range(j + 1, 8):
            for i in range(k, 8):
                block[i][k] = block[i][k] - factors[i] * factors[k]
        if count:
            multiplier = columns[j] * inverse[None]
            for k in range(j + 1, 8):
                columns[k] = columns[k] - multiplier * factors[k][None]
            multipliers.append(multiplier)
        row = jnp.broadcast_to(work[at + j : at + j + 1, :], (8, width))
        for q in range(j):
            row = row - across(lower[q][j], width) * scaled_rows[q]
        row = row * across(inverse, width)
        lower.append(factors)
        scaled_rows.append(row)
        result = row if result is None else jnp.where(sub >= j, row, result)
    work[at : at + 8, :] = result
    for t in range(count):
        rows = work[at + 8 + 8 * t : at + 16 + 8 * t, :]
        for j in range(8):
            rows = rows - across(multipliers[j][t], width) * scaled_rows[j]
        work[at + 8 + 8 * t : at + 16 + 8 * t, :] = rows
    if at + 8 == end and end < K:
        group = work[end - NB : end, :]
        work[end:, :] = work[end:, :] - tn_thin(group[:, end:K], group)


def eliminate(*works):
    for at in range(0, K, 8):
        for work in works:
            eliminate_rows(work, at)


def leaf_kernel(parts, sketched, panel, gram, work_z, work_h):
    work_h[...] = jnp.sum(parts[:, :K, :], axis=0)
    for part in range(PIX):
        work_z[16 * part : 16 * (part + 1), :K] = parts[part, K:, :]
    row_at = lax.broadcasted_iota(jnp.int32, (K, K), 0)
    col_at = lax.broadcasted_iota(jnp.int32, (K, K), 1)
    work_z[:, K:] = jnp.where(row_at == col_at, 1.0, 0.0)
    eliminate(work_z, work_h)
    inverse = work_z[:, K:]
    factor = nt(inverse, jnp.where(col_at >= row_at, work_h[...], 0.0))
    panel[...] = nn(sketched[...], tn(inverse, factor))
    gram[...] = tn(factor, factor)


def joined(gram, front_gram, cross, back_gram):
    largest = jnp.maximum(
        jnp.max(front_gram, keepdims=True), jnp.max(back_gram, keepdims=True)
    )
    scale = 1.0 / largest
    gram[:K, :K] = front_gram * scale
    gram[:K, K:] = cross * scale
    gram[K:, :K] = cross.T * scale
    gram[K:, K:] = back_gram * scale
    return largest, scale


def prepared(gram, work, last):
    powered = nn(gram[:K, :], gram[...])
    if last:
        work[:, :K] = nt(nn(powered, gram[...]), powered)
    else:
        work[:, :K] = nt(powered, powered)
    work[:, K:] = powered


def merge_kernel(core, keys, mine, other, own_gram, partner_gram, front, back, out, merged, gram, work):
    rows = front.shape[0]
    half = K // 2
    second = core[:1, :] > 0.5
    lead = keys[:1, :] < keys[8:9, :]
    top = jnp.where(second, other[...], mine[...])
    low = jnp.where(second, mine[...], other[...])
    largest, _ = joined(
        gram,
        jnp.where(lead, own_gram[...], partner_gram[...]),
        jnp.concatenate([top, low], axis=0),
        jnp.where(lead, partner_gram[...], own_gram[...]),
    )
    prepared(gram, work, False)
    eliminate(work)
    rotation = work[:, K:]
    out[:rows, :] = nt(front[...], rotation[:, :K]) + nt(back[...], rotation[:, K:])
    fresh = nt(nn(rotation, gram[...]), rotation) * largest
    merged[...] = fresh
    out[rows : rows + half, :] = jnp.where(second, fresh[half:, :], fresh[:half, :])
    out[rows + half :, :] = jnp.minimum(keys[:8, :], keys[8:, :])


PAIRS = ((0, 1), (2, 3), (0, 2), (0, 3), (1, 2), (1, 3))


def quad_kernel(last, core, mine, other, panels, *refs):
    out, (gram_a, gram_b, work_a, work_b) = refs[0], refs[-4:]
    half = K // 2
    shares = 3 * K
    rows = panels.shape[1] - half - 8
    second = core[:1, :] > 0.5

    def gram_of(i):
        own = panels[i, rows : rows + half, :]
        got = other[shares + half * i : shares + half * (i + 1), :]
        return jnp.concatenate(
            [jnp.where(second, got, own), jnp.where(second, own, got)], axis=0
        )

    def cross_of(pair):
        at = PAIRS.index(pair)
        share, lane = divmod(at, 3)
        span = slice(lane * K, lane * K + K)
        if share == 0:
            return jnp.where(second, other[span, :], mine[span, :])
        return jnp.where(second, mine[span, :], other[span, :])

    def key_of(i):
        return panels[i, rows + half : rows + half + 1, :]

    def ordered(lead, first_gram, cross, second_gram, gram):
        return joined(
            gram,
            jnp.where(lead, first_gram, second_gram),
            jnp.where(lead, cross, cross.T),
            jnp.where(lead, second_gram, first_gram),
        )

    def parted(lead, rotation):
        left, right = rotation[:, :K], rotation[:, K:]
        return jnp.where(lead, left, right), jnp.where(lead, right, left)

    lead_a, lead_b = key_of(0) < key_of(1), key_of(2) < key_of(3)
    largest_a, _ = ordered(lead_a, gram_of(0), cross_of((0, 1)), gram_of(1), gram_a)
    largest_b, _ = ordered(lead_b, gram_of(2), cross_of((2, 3)), gram_of(3), gram_b)
    prepared(gram_a, work_a, False)
    prepared(gram_b, work_b, False)
    eliminate(work_a, work_b)
    rotation_a, rotation_b = work_a[:, K:], work_b[:, K:]
    merged_a = nt(nn(rotation_a, gram_a[...]), rotation_a) * largest_a
    merged_b = nt(nn(rotation_b, gram_b[...]), rotation_b) * largest_b
    part_0, part_1 = parted(lead_a, rotation_a)
    part_2, part_3 = parted(lead_b, rotation_b)
    mixed_2 = nn(part_0, cross_of((0, 2))) + nn(part_1, cross_of((1, 2)))
    mixed_3 = nn(part_0, cross_of((0, 3))) + nn(part_1, cross_of((1, 3)))
    cross = nt(mixed_2, part_2) + nt(mixed_3, part_3)
    key_a = jnp.minimum(key_of(0), key_of(1))
    key_b = jnp.minimum(key_of(2), key_of(3))
    lead = key_a < key_b
    largest, scale = ordered(lead, merged_a, cross, merged_b, gram_a)
    prepared(gram_a, work_a, last)
    eliminate(work_a)
    rotation = work_a[:, K:]
    left, right = parted(lead, rotation)
    panel = nt(panels[0, :rows, :], nn(left, part_0))
    panel = panel + nt(panels[1, :rows, :], nn(left, part_1))
    panel = panel + nt(panels[2, :rows, :], nn(right, part_2))
    panel = panel + nt(panels[3, :rows, :], nn(right, part_3))
    if last:
        out[...] = panel * (math.sqrt(NPIX) * jnp.sqrt(scale))
    else:
        out[:rows, :] = panel
        fresh = nt(nn(rotation, gram_a[...]), rotation) * largest
        out[rows : rows + half, :] = jnp.where(second, fresh[half:, :], fresh[:half, :])
        out[rows + half :, :] = jnp.broadcast_to(jnp.minimum(key_a, key_b), (8, K))


def swapped(block, axis, bit):
    count = lax.axis_size(axis)
    return lax.ppermute(block, axis, [(low, low ^ 1 << bit) for low in range(count)])


def spread(block):
    many = jnp.broadcast_to(block[None], (PIX,) + block.shape)
    return lax.all_to_all(many, "pix", 0, 0)


def per_device(spectra, sketch, block_mask, rank_key):
    batch, width = spectra.shape
    share = batch // PIX
    rows = width // 2
    half = K // 2
    second = lax.axis_index("gal") % 2 == 1
    core_rows = jnp.broadcast_to(second.astype(jnp.float32), (8, K))
    pixel_mask = jnp.repeat(block_mask[0], width // block_mask.shape[1]).astype(jnp.bfloat16)
    masked = spectra * pixel_mask[None, :]
    sketched = lax.dot_general(
        masked, sketch, (((0,), (0,)), ((), ())), preferred_element_type=jnp.float32
    )
    sketch_gram = tn(sketched, sketched)
    high = lax.reduce_precision(sketched, 8, 7)
    low = sketched - high
    pieces = jnp.concatenate([high.astype(jnp.bfloat16), low.astype(jnp.bfloat16)], axis=1)
    both = jnp.dot(masked, pieces, preferred_element_type=jnp.float32)
    projected = both[:, :K] + both[:, K:]
    sends = jnp.concatenate(
        [projected.reshape(PIX, share, K), sketch_gram.reshape(PIX, K // PIX, K)], axis=1
    )
    summed = jnp.sum(lax.all_to_all(sends, "pix", 0, 0), axis=0)
    own_rows = summed[:share]
    parts = spread(jnp.concatenate([tn(own_rows, own_rows), summed[share:]], axis=0))
    leaf_panel, own_gram = pl.pallas_call(
        leaf_kernel,
        out_shape=[
            jax.ShapeDtypeStruct((width, K), jnp.float32),
            jax.ShapeDtypeStruct((K, K), jnp.float32),
        ],
        scratch_shapes=[pltpu.VMEM((K, 2 * K), jnp.float32), pltpu.VMEM((K, K), jnp.float32)],
        compiler_params=PARAMS,
        name="leaf",
    )(parts, sketched)
    key_rows = jnp.broadcast_to(rank_key.astype(jnp.float32)[:, None], (8, K))
    kept = jnp.where(second, leaf_panel[rows:], leaf_panel[:rows])
    sent = jnp.where(second, leaf_panel[:rows], leaf_panel[rows:])
    got = swapped(jnp.concatenate([sent, own_gram, key_rows], axis=0), "gal", 0)
    other_panel, partner_gram, other_key = got[:rows], got[rows : rows + K], got[rows + K :]
    for level in range(2):
        if level:
            got = swapped(state, "gal", level)
            kept, key_rows = state[:rows], state[rows + half :]
            other_panel, other_key = got[:rows], got[rows + half :]
        lead = key_rows[:1] < other_key[:1]
        front = jnp.where(lead, kept, other_panel)
        back = jnp.where(lead, other_panel, kept)
        cross = tn(front, back)
        cross_sent = jnp.where(second, cross[:half], cross[half:])
        cross_kept = jnp.where(second, cross[half:], cross[:half])
        mine = jnp.sum(spread(cross_kept + swapped(cross_sent, "gal", 0)), axis=0)
        if level:
            gram_half = got[rows : rows + half]
            other = swapped(jnp.concatenate([mine, gram_half], axis=0), "gal", 0)
            other, other_half = other[:half], other[half:]
            partner_gram = jnp.concatenate(
                [
                    jnp.where(second, other_half, gram_half),
                    jnp.where(second, gram_half, other_half),
                ],
                axis=0,
            )
        else:
            other = swapped(mine, "gal", 0)
        keys = jnp.concatenate([key_rows, other_key], axis=0)
        state, own_gram = pl.pallas_call(
            merge_kernel,
            out_shape=[
                jax.ShapeDtypeStruct((rows + half + 8, K), jnp.float32),
                jax.ShapeDtypeStruct((K, K), jnp.float32),
            ],
            scratch_shapes=[
                pltpu.VMEM((2 * K, 2 * K), jnp.float32),
                pltpu.VMEM((K, 3 * K), jnp.float32),
            ],
            compiler_params=PARAMS,
            name="merge",
        )(core_rows, keys, mine, other, own_gram, partner_gram, front, back)
    count = lax.axis_size("gal")
    for level in (2, 4):
        last = level == 4
        groups = [
            [base + (part << level) for part in range(4)]
            for base in range(count)
            if not base >> level & 3
        ]
        panels = lax.all_to_all(
            jnp.broadcast_to(state[None], (4,) + state.shape),
            "gal",
            0,
            0,
            axis_index_groups=groups,
        )
        cross = jnp.concatenate(
            [tn(panels[i, :rows], panels[j, :rows]) for i, j in PAIRS], axis=0
        )
        cross_sent = jnp.where(second, cross[: 3 * K], cross[3 * K :])
        cross_kept = jnp.where(second, cross[3 * K :], cross[: 3 * K])
        cross = cross_kept + swapped(cross_sent, "gal", 0)
        own = jnp.sum(lax.all_to_all(cross.reshape(PIX, -1, K), "pix", 0, 0), axis=0)
        mine = spread(own).reshape(3 * K, K)
        halves = panels[:, rows : rows + half].reshape(4 * half, K)
        other = swapped(jnp.concatenate([mine, halves], axis=0), "gal", 0)
        state = pl.pallas_call(
            functools.partial(quad_kernel, last),
            out_shape=jax.ShapeDtypeStruct((rows if last else rows + half + 8, K), jnp.float32),
            scratch_shapes=[
                pltpu.VMEM((2 * K, 2 * K), jnp.float32),
                pltpu.VMEM((2 * K, 2 * K), jnp.float32),
                pltpu.VMEM((K, 3 * K), jnp.float32),
                pltpu.VMEM((K, 3 * K), jnp.float32),
            ],
            compiler_params=PARAMS,
            name="finish" if last else "quad",
        )(core_rows, mine, other, panels)
    other = swapped(state, "gal", 0)
    basis = jnp.concatenate(
        [jnp.where(second, other, state), jnp.where(second, state, other)], axis=0
    )
    score_terms = jnp.dot(masked, basis.astype(jnp.bfloat16), preferred_element_type=jnp.float32)
    own_scores = jnp.sum(
        lax.all_to_all(score_terms.reshape(PIX, share, K), "pix", 0, 0), axis=0
    )
    scores = spread(own_scores * (1.0 / NPIX)).reshape(batch, K)
    return (basis, scores)


def solution(mesh):
    in_specs = (P("gal", "pix"), P("gal", None), P("gal", "pix"), P("gal"))
    out_specs = (P("pix", None), P("gal", None))
    return jax.shard_map(
        per_device, mesh=mesh, in_specs=in_specs, out_specs=out_specs, check_vma=False
    )
```

```python
import functools
import math

import jax
import jax.numpy as jnp
from jax import lax
from jax.experimental import pallas as pl
from jax.experimental.pallas import tpu as pltpu
from jax.sharding import PartitionSpec as P

NPIX = 8192
K = 128
PIX = 8
HIGH = lax.Precision.HIGHEST
PARAMS = pltpu.CompilerParams(vmem_limit_bytes=32 * 1024 * 1024)
NB = 32
LANES = 128
ROWS = 128


def dot_of(a, b, dims):
    return lax.dot_general(
        a, b, (dims, ((), ())), precision=HIGH, preferred_element_type=jnp.float32
    )


def nn(a, b):
    return dot_of(a, b, ((1,), (0,)))


def nt(a, b):
    return dot_of(a, b, ((1,), (1,)))


def tn(a, b):
    return dot_of(a, b, ((0,), (0,)))


def split3(x):
    high = x.astype(jnp.bfloat16)
    rest = x - high.astype(jnp.float32)
    middle = rest.astype(jnp.bfloat16)
    low = (rest - middle.astype(jnp.float32)).astype(jnp.bfloat16)
    return high, middle, low


def tn_thin(a, b):
    ah, am, al = split3(a)
    bh, bm, bl = split3(b)
    left = jnp.concatenate([ah, ah, am, am, ah, al], axis=0)
    right = jnp.concatenate([bh, bm, bh, bm, bl, bh], axis=0)
    return lax.dot_general(
        left, right, (((0,), (0,)), ((), ())), preferred_element_type=jnp.float32
    )


def whole(x):
    return jnp.broadcast_to(x, (8, LANES))


def across(x, width):
    return jnp.concatenate([x] * (width // LANES), axis=1)


def eliminate_rows(work, at):
    width = work.shape[1]
    end = (at // NB + 1) * NB
    count = (end - at) // 8 - 1
    sub = lax.broadcasted_iota(jnp.int32, (8, width), 0)
    pivots = [jnp.broadcast_to(work[at + i : at + i + 1, :K], (8, K)) for i in range(8)]
    block = [[whole(pivots[i][:, at + k : at + k + 1]) for k in range(i + 1)] for i in range(8)]
    columns = None
    if count:
        columns = [
            jnp.broadcast_to(work[at + 8 : end, at + k : at + k + 1], (8 * count, LANES)).reshape(
                count, 8, LANES
            )
            for k in range(8)
        ]
    lower, scaled_rows, multipliers = [], [], []
    result = None
    for j in range(8):
        inverse = lax.rsqrt(block[j][j])
        factors = [block[i][j] * inverse if i > j else None for i in range(8)]
        for k in range(j + 1, 8):
            for i in range(k, 8):
                block[i][k] = block[i][k] - factors[i] * factors[k]
        if count:
            multiplier = columns[j] * inverse[None]
            for k in range(j + 1, 8):
                columns[k] = columns[k] - multiplier * factors[k][None]
            multipliers.append(multiplier)
        row = jnp.broadcast_to(work[at + j : at + j + 1, :], (8, width))
        for q in range(j):
            row = row - across(lower[q][j], width) * scaled_rows[q]
        row = row * across(inverse, width)
        lower.append(factors)
        scaled_rows.append(row)
        result = row if result is None else jnp.where(sub >= j, row, result)
    work[at : at + 8, :] = result
    for t in range(count):
        rows = work[at + 8 + 8 * t : at + 16 + 8 * t, :]
        for j in range(8):
            rows = rows - across(multipliers[j][t], width) * scaled_rows[j]
        work[at + 8 + 8 * t : at + 16 + 8 * t, :] = rows
    if at + 8 == end and end < K:
        group = work[end - NB : end, :]
        work[end:, :] = work[end:, :] - tn_thin(group[:, end:K], group)


def eliminate(*works):
    for at in range(0, K, 8):
        for work in works:
            eliminate_rows(work, at)


def leaf_kernel(parts, out, work_z, work_h):
    share = parts.shape[1] - 2 * K // PIX
    step = K // PIX
    summed = parts[:, :share, :].reshape(PIX * share, K)
    work_h[...] = tn(summed, summed)
    for part in range(PIX):
        span = slice(step * part, step * (part + 1))
        work_z[span, :K] = parts[part, share : share + step, :]
        out[2 * K + step * part : 2 * K + step * (part + 1), :] = parts[part, share + step :, :]
    row_at = lax.broadcasted_iota(jnp.int32, (K, K), 0)
    col_at = lax.broadcasted_iota(jnp.int32, (K, K), 1)
    work_z[:, K:] = jnp.where(row_at == col_at, 1.0, 0.0)
    eliminate(work_z, work_h)
    inverse = work_z[:, K:]
    factor = nt(inverse, jnp.where(col_at >= row_at, work_h[...], 0.0))
    out[:K, :] = tn(inverse, factor)
    out[K : 2 * K, :] = tn(factor, factor)


def joined(gram, front_gram, cross, back_gram):
    largest = jnp.maximum(
        jnp.max(front_gram, keepdims=True), jnp.max(back_gram, keepdims=True)
    )
    scale = 1.0 / largest
    gram[:K, :K] = front_gram * scale
    gram[:K, K:] = cross * scale
    gram[K:, :K] = cross.T * scale
    gram[K:, K:] = back_gram * scale
    return largest, scale


def prepared(gram, work, last):
    powered = nn(gram[:K, :], gram[...])
    if last:
        work[:, :K] = nt(nn(powered, gram[...]), powered)
    else:
        work[:, :K] = nt(powered, powered)
    work[:, K:] = powered


def finish_pair(lead, core, keys, front, back, coefficients, largest, out, merged, gram, work):
    rows = front.shape[0]
    half = K // 2
    second = core[:1, :] > 0.5
    prepared(gram, work, False)
    eliminate(work)
    rotation = work[:, K:]
    if coefficients is None:
        out[:rows, :] = nt(front[...], rotation[:, :K]) + nt(back[...], rotation[:, K:])
    else:
        left, right = coefficients
        out[:rows, :] = nn(front[...], nt(left, rotation[:, :K])) + nn(
            back[...], nt(right, rotation[:, K:])
        )
    fresh = nt(nn(rotation, gram[...]), rotation) * largest
    merged[...] = fresh
    out[rows : rows + half, :] = jnp.where(second, fresh[half:, :], fresh[:half, :])
    out[rows + half :, :] = jnp.minimum(keys[:8, :], keys[8:, :])


def first_kernel(core, keys, own, other, front, back, out, merged, gram, work):
    lead = keys[:1, :] < keys[8:9, :]
    left = jnp.where(lead, own[:K, :], other[:K, :])
    right = jnp.where(lead, other[:K, :], own[:K, :])
    cross = own[2 * K :, :] + other[2 * K :, :]
    largest, _ = joined(
        gram,
        jnp.where(lead, own[K : 2 * K, :], other[K : 2 * K, :]),
        nn(tn(left, cross), right),
        jnp.where(lead, other[K : 2 * K, :], own[K : 2 * K, :]),
    )
    finish_pair(lead, core, keys, front, back, (left, right), largest, out, merged, gram, work)


def merge_kernel(core, keys, mine, other, own_gram, partner_gram, front, back, *refs):
    out, merged, gram, work = refs
    second = core[:1, :] > 0.5
    lead = keys[:1, :] < keys[8:9, :]
    top = jnp.where(second, other[...], mine[...])
    low = jnp.where(second, mine[...], other[...])
    largest, _ = joined(
        gram,
        jnp.where(lead, own_gram[...], partner_gram[...]),
        jnp.concatenate([top, low], axis=0),
        jnp.where(lead, partner_gram[...], own_gram[...]),
    )
    finish_pair(lead, core, keys, front, back, None, largest, out, merged, gram, work)


PAIRS = ((0, 1), (2, 3), (0, 2), (0, 3), (1, 2), (1, 3))


def cross_kernel(panels, out):
    for at, (i, j) in enumerate(PAIRS):
        out[K * at : K * (at + 1), :] = tn(panels[i, :ROWS, :], panels[j, :ROWS, :])


def quad_kernel(last, core, crosses, halves, panels, *refs):
    out, (gram_a, gram_b, work_a, work_b) = refs[0], refs[-4:]
    half = K // 2
    rows = ROWS
    second = core[:1, :] > 0.5

    def gram_of(i):
        own = panels[i, rows : rows + half, :]
        got = halves[half * i : half * (i + 1), :]
        return jnp.concatenate(
            [jnp.where(second, got, own), jnp.where(second, own, got)], axis=0
        )

    def cross_of(pair):
        at = PAIRS.index(pair)
        return crosses[K * at : K * (at + 1), :]

    def key_of(i):
        return panels[i, rows + half : rows + half + 1, :]

    def ordered(lead, first_gram, cross, second_gram, gram):
        return joined(
            gram,
            jnp.where(lead, first_gram, second_gram),
            jnp.where(lead, cross, cross.T),
            jnp.where(lead, second_gram, first_gram),
        )

    def parted(lead, rotation):
        left, right = rotation[:, :K], rotation[:, K:]
        return jnp.where(lead, left, right), jnp.where(lead, right, left)

    lead_a, lead_b = key_of(0) < key_of(1), key_of(2) < key_of(3)
    largest_a, _ = ordered(lead_a, gram_of(0), cross_of((0, 1)), gram_of(1), gram_a)
    largest_b, _ = ordered(lead_b, gram_of(2), cross_of((2, 3)), gram_of(3), gram_b)
    prepared(gram_a, work_a, False)
    prepared(gram_b, work_b, False)
    eliminate(work_a, work_b)
    rotation_a, rotation_b = work_a[:, K:], work_b[:, K:]
    merged_a = nt(nn(rotation_a, gram_a[...]), rotation_a) * largest_a
    merged_b = nt(nn(rotation_b, gram_b[...]), rotation_b) * largest_b
    part_0, part_1 = parted(lead_a, rotation_a)
    part_2, part_3 = parted(lead_b, rotation_b)
    mixed_2 = nn(part_0, cross_of((0, 2))) + nn(part_1, cross_of((1, 2)))
    mixed_3 = nn(part_0, cross_of((0, 3))) + nn(part_1, cross_of((1, 3)))
    cross = nt(mixed_2, part_2) + nt(mixed_3, part_3)
    key_a = jnp.minimum(key_of(0), key_of(1))
    key_b = jnp.minimum(key_of(2), key_of(3))
    lead = key_a < key_b
    largest, scale = ordered(lead, merged_a, cross, merged_b, gram_a)
    prepared(gram_a, work_a, last)
    eliminate(work_a)
    rotation = work_a[:, K:]
    left, right = parted(lead, rotation)
    panel = nt(panels[0, :rows, :], nn(left, part_0))
    panel = panel + nt(panels[1, :rows, :], nn(left, part_1))
    panel = panel + nt(panels[2, :rows, :], nn(right, part_2))
    panel = panel + nt(panels[3, :rows, :], nn(right, part_3))
    if last:
        out[...] = panel * (math.sqrt(NPIX) * jnp.sqrt(scale))
    else:
        out[:rows, :] = panel
        fresh = nt(nn(rotation, gram_a[...]), rotation) * largest
        out[rows : rows + half, :] = jnp.where(second, fresh[half:, :], fresh[:half, :])
        out[rows + half :, :] = jnp.broadcast_to(jnp.minimum(key_a, key_b), (8, K))


def swapped(block, axis, bit):
    count = lax.axis_size(axis)
    return lax.ppermute(block, axis, [(low, low ^ 1 << bit) for low in range(count)])


def spread(block):
    many = jnp.broadcast_to(block[None], (PIX,) + block.shape)
    return lax.all_to_all(many, "pix", 0, 0)


def per_device(spectra, sketch, block_mask, rank_key):
    batch, width = spectra.shape
    share = batch // PIX
    rows = width // 2
    half = K // 2
    second = lax.axis_index("gal") % 2 == 1
    core_rows = jnp.broadcast_to(second.astype(jnp.float32), (8, K))
    pixel_mask = jnp.repeat(block_mask[0], width // block_mask.shape[1]).astype(jnp.bfloat16)
    masked = spectra * pixel_mask[None, :]
    sketched = lax.dot_general(
        masked, sketch, (((0,), (0,)), ((), ())), preferred_element_type=jnp.float32
    )
    sketch_gram = tn(sketched, sketched)
    key_rows = jnp.broadcast_to(rank_key.astype(jnp.float32)[:, None], (8, K))
    kept = jnp.where(second, sketched[rows:], sketched[:rows])
    sent = jnp.where(second, sketched[:rows], sketched[rows:])
    got = swapped(jnp.concatenate([sent, key_rows], axis=0), "gal", 0)
    high = lax.reduce_precision(sketched, 8, 7)
    low = sketched - high
    pieces = jnp.concatenate([high.astype(jnp.bfloat16), low.astype(jnp.bfloat16)], axis=1)
    both = jnp.dot(masked, pieces, preferred_element_type=jnp.float32)
    projected = both[:, :K] + both[:, K:]
    lead = key_rows[:1] < got[rows : rows + 1]
    front = jnp.where(lead, kept, got[:rows])
    back = jnp.where(lead, got[:rows], kept)
    sends = jnp.concatenate(
        [
            projected.reshape(PIX, share, K),
            sketch_gram.reshape(PIX, K // PIX, K),
            tn(front, back).reshape(PIX, K // PIX, K),
        ],
        axis=1,
    )
    parts = spread(jnp.sum(lax.all_to_all(sends, "pix", 0, 0), axis=0))
    own = pl.pallas_call(
        leaf_kernel,
        out_shape=jax.ShapeDtypeStruct((3 * K, K), jnp.float32),
        scratch_shapes=[pltpu.VMEM((K, 2 * K), jnp.float32), pltpu.VMEM((K, K), jnp.float32)],
        compiler_params=PARAMS,
        name="leaf",
    )(parts)
    pair_out = [
        jax.ShapeDtypeStruct((rows + half + 8, K), jnp.float32),
        jax.ShapeDtypeStruct((K, K), jnp.float32),
    ]
    pair_scratch = [
        pltpu.VMEM((2 * K, 2 * K), jnp.float32),
        pltpu.VMEM((K, 3 * K), jnp.float32),
    ]
    state, own_gram = pl.pallas_call(
        first_kernel,
        out_shape=pair_out,
        scratch_shapes=pair_scratch,
        compiler_params=PARAMS,
        name="first",
    )(
        core_rows,
        jnp.concatenate([key_rows, got[rows:]], axis=0),
        own,
        swapped(own, "gal", 0),
        front,
        back,
    )
    got = swapped(state, "gal", 1)
    kept, key_rows = state[:rows], state[rows + half :]
    lead = key_rows[:1] < got[rows + half : rows + half + 1]
    front = jnp.where(lead, kept, got[:rows])
    back = jnp.where(lead, got[:rows], kept)
    cross = tn(front, back)
    cross_sent = jnp.where(second, cross[:half], cross[half:])
    cross_kept = jnp.where(second, cross[half:], cross[:half])
    mine = jnp.sum(spread(cross_kept + swapped(cross_sent, "gal", 0)), axis=0)
    gram_half = got[rows : rows + half]
    other = swapped(jnp.concatenate([mine, gram_half], axis=0), "gal", 0)
    partner_gram = jnp.concatenate(
        [
            jnp.where(second, other[half:], gram_half),
            jnp.where(second, gram_half, other[half:]),
        ],
        axis=0,
    )
    state, own_gram = pl.pallas_call(
        merge_kernel,
        out_shape=pair_out,
        scratch_shapes=pair_scratch,
        compiler_params=PARAMS,
        name="merge",
    )(
        core_rows,
        jnp.concatenate([key_rows, got[rows + half :]], axis=0),
        mine,
        other[:half],
        own_gram,
        partner_gram,
        front,
        back,
    )
    count = lax.axis_size("gal")
    holders = [core + (part << 2) for core in range(2) for part in range(4)]
    eights = [[base + at for at in holders] for base in range(count) if not base & 13]
    everyone = [[at * PIX + pix for at in eight for pix in range(PIX)] for eight in eights]
    for level in (2, 4):
        last = level == 4
        groups = [
            [base + (part << level) for part in range(4)]
            for base in range(count)
            if not base >> level & 3
        ]
        if level == 2:
            tail = jnp.broadcast_to(state[None, rows:], (4, half + 8, K))
            sends = jnp.concatenate([state[:rows].reshape(4, ROWS, K), tail], axis=1)
        else:
            sends = jnp.broadcast_to(state[None], (4,) + state.shape)
        panels = lax.all_to_all(sends, "gal", 0, 0, axis_index_groups=groups)
        halves = swapped(panels[:, ROWS : ROWS + half].reshape(4 * half, K), "gal", 0)
        cross = pl.pallas_call(
            cross_kernel,
            out_shape=jax.ShapeDtypeStruct((len(PAIRS) * K, K), jnp.float32),
            compiler_params=PARAMS,
            name="cross",
        )(panels)
        size = len(everyone[0])
        own = jnp.sum(
            lax.all_to_all(
                cross.reshape(size, -1, K), ("gal", "pix"), 0, 0, axis_index_groups=everyone
            ),
            axis=0,
        )
        crosses = lax.all_to_all(
            jnp.broadcast_to(own[None], (size,) + own.shape),
            ("gal", "pix"),
            0,
            0,
            axis_index_groups=everyone,
        ).reshape(cross.shape)
        state = pl.pallas_call(
            functools.partial(quad_kernel, last),
            out_shape=jax.ShapeDtypeStruct((ROWS if last else ROWS + half + 8, K), jnp.float32),
            scratch_shapes=pair_scratch[:1] * 2 + pair_scratch[1:] * 2,
            compiler_params=PARAMS,
            name="finish" if last else "quad",
        )(core_rows, crosses, halves, panels)
    basis = lax.all_to_all(
        jnp.broadcast_to(state[None], (8, ROWS, K)), "gal", 0, 0, axis_index_groups=eights
    ).reshape(width, K)
    score_terms = jnp.dot(masked, basis.astype(jnp.bfloat16), preferred_element_type=jnp.float32)
    own_scores = jnp.sum(
        lax.all_to_all(score_terms.reshape(PIX, share, K), "pix", 0, 0), axis=0
    )
    scores = spread(own_scores * (1.0 / NPIX)).reshape(batch, K)
    return (basis, scores)


def solution(mesh):
    in_specs = (P("gal", "pix"), P("gal", None), P("gal", "pix"), P("gal"))
    out_specs = (P("pix", None), P("gal", None))
    return jax.shard_map(
        per_device, mesh=mesh, in_specs=in_specs, out_specs=out_specs, check_vma=False
    )
```

```python
import functools
import math

import jax
import jax.numpy as jnp
from jax import lax
from jax.experimental import pallas as pl
from jax.experimental.pallas import tpu as pltpu
from jax.sharding import PartitionSpec as P

NPIX = 8192
K = 128
PIX = 8
HIGH = lax.Precision.HIGHEST
PARAMS = pltpu.CompilerParams(vmem_limit_bytes=32 * 1024 * 1024)
NB = 32
LANES = 128


def dot_of(a, b, dims):
    return lax.dot_general(
        a, b, (dims, ((), ())), precision=HIGH, preferred_element_type=jnp.float32
    )


def nn(a, b):
    return dot_of(a, b, ((1,), (0,)))


def nt(a, b):
    return dot_of(a, b, ((1,), (1,)))


def tn(a, b):
    return dot_of(a, b, ((0,), (0,)))


def split3(x):
    high = x.astype(jnp.bfloat16)
    rest = x - high.astype(jnp.float32)
    middle = rest.astype(jnp.bfloat16)
    low = (rest - middle.astype(jnp.float32)).astype(jnp.bfloat16)
    return high, middle, low


def tn_thin(a, b):
    ah, am, al = split3(a)
    bh, bm, bl = split3(b)
    left = jnp.concatenate([ah, ah, am, am, ah, al], axis=0)
    right = jnp.concatenate([bh, bm, bh, bm, bl, bh], axis=0)
    return lax.dot_general(
        left, right, (((0,), (0,)), ((), ())), preferred_element_type=jnp.float32
    )


def whole(x):
    return jnp.broadcast_to(x, (8, LANES))


def across(x, width):
    return jnp.concatenate([x] * (width // LANES), axis=1)


def eliminate_rows(work, at):
    width = work.shape[1]
    end = (at // NB + 1) * NB
    count = (end - at) // 8 - 1
    sub = lax.broadcasted_iota(jnp.int32, (8, width), 0)
    pivots = [jnp.broadcast_to(work[at + i : at + i + 1, :K], (8, K)) for i in range(8)]
    block = [[whole(pivots[i][:, at + k : at + k + 1]) for k in range(i + 1)] for i in range(8)]
    columns = None
    if count:
        columns = [
            jnp.broadcast_to(work[at + 8 : end, at + k : at + k + 1], (8 * count, LANES)).reshape(
                count, 8, LANES
            )
            for k in range(8)
        ]
    lower, scaled_rows, multipliers = [], [], []
    result = None
    for j in range(8):
        inverse = lax.rsqrt(block[j][j])
        factors = [block[i][j] * inverse if i > j else None for i in range(8)]
        for k in range(j + 1, 8):
            for i in range(k, 8):
                block[i][k] = block[i][k] - factors[i] * factors[k]
        if count:
            multiplier = columns[j] * inverse[None]
            for k in range(j + 1, 8):
                columns[k] = columns[k] - multiplier * factors[k][None]
            multipliers.append(multiplier)
        row = jnp.broadcast_to(work[at + j : at + j + 1, :], (8, width))
        for q in range(j):
            row = row - across(lower[q][j], width) * scaled_rows[q]
        row = row * across(inverse, width)
        lower.append(factors)
        scaled_rows.append(row)
        result = row if result is None else jnp.where(sub >= j, row, result)
    work[at : at + 8, :] = result
    for t in range(count):
        rows = work[at + 8 + 8 * t : at + 16 + 8 * t, :]
        for j in range(8):
            rows = rows - across(multipliers[j][t], width) * scaled_rows[j]
        work[at + 8 + 8 * t : at + 16 + 8 * t, :] = rows
    if at + 8 == end and end < K:
        group = work[end - NB : end, :]
        work[end:, :] = work[end:, :] - tn_thin(group[:, end:K], group)


def eliminate(*works):
    for at in range(0, K, 8):
        for work in works:
            eliminate_rows(work, at)


def leaf_kernel(parts, out, work_z, work_h):
    share = parts.shape[1] - 2 * K // PIX
    step = K // PIX
    summed = parts[:, :share, :].reshape(PIX * share, K)
    work_h[...] = tn(summed, summed)
    for part in range(PIX):
        span = slice(step * part, step * (part + 1))
        work_z[span, :K] = parts[part, share : share + step, :]
        out[2 * K + step * part : 2 * K + step * (part + 1), :] = parts[part, share + step :, :]
    row_at = lax.broadcasted_iota(jnp.int32, (K, K), 0)
    col_at = lax.broadcasted_iota(jnp.int32, (K, K), 1)
    work_z[:, K:] = jnp.where(row_at == col_at, 1.0, 0.0)
    eliminate(work_z, work_h)
    inverse = work_z[:, K:]
    factor = nt(inverse, jnp.where(col_at >= row_at, work_h[...], 0.0))
    out[:K, :] = tn(inverse, factor)
    out[K : 2 * K, :] = tn(factor, factor)


def joined(gram, front_gram, cross, back_gram):
    largest = jnp.maximum(
        jnp.max(front_gram, keepdims=True), jnp.max(back_gram, keepdims=True)
    )
    scale = 1.0 / largest
    gram[:K, :K] = front_gram * scale
    gram[:K, K:] = cross * scale
    gram[K:, :K] = cross.T * scale
    gram[K:, K:] = back_gram * scale
    return largest, scale


def prepared(gram, work, last):
    powered = nn(gram[:K, :], gram[...])
    if last:
        work[:, :K] = nt(nn(powered, gram[...]), powered)
    else:
        work[:, :K] = nt(powered, powered)
    work[:, K:] = powered


def finish_pair(lead, core, keys, front, back, coefficients, largest, out, merged, gram, work):
    rows = front.shape[0]
    half = K // 2
    second = core[:1, :] > 0.5
    prepared(gram, work, False)
    eliminate(work)
    rotation = work[:, K:]
    if coefficients is None:
        out[:rows, :] = nt(front[...], rotation[:, :K]) + nt(back[...], rotation[:, K:])
    else:
        left, right = coefficients
        out[:rows, :] = nn(front[...], nt(left, rotation[:, :K])) + nn(
            back[...], nt(right, rotation[:, K:])
        )
    fresh = nt(nn(rotation, gram[...]), rotation) * largest
    merged[...] = fresh
    out[rows : rows + half, :] = jnp.where(second, fresh[half:, :], fresh[:half, :])
    out[rows + half :, :] = jnp.minimum(keys[:8, :], keys[8:, :])


def first_kernel(core, keys, own, other, front, back, out, merged, gram, work):
    lead = keys[:1, :] < keys[8:9, :]
    left = jnp.where(lead, own[:K, :], other[:K, :])
    right = jnp.where(lead, other[:K, :], own[:K, :])
    cross = own[2 * K :, :] + other[2 * K :, :]
    largest, _ = joined(
        gram,
        jnp.where(lead, own[K : 2 * K, :], other[K : 2 * K, :]),
        nn(tn(left, cross), right),
        jnp.where(lead, other[K : 2 * K, :], own[K : 2 * K, :]),
    )
    finish_pair(lead, core, keys, front, back, (left, right), largest, out, merged, gram, work)


def merge_kernel(core, keys, mine, other, own_gram, partner_gram, front, back, *refs):
    out, merged, gram, work = refs
    second = core[:1, :] > 0.5
    lead = keys[:1, :] < keys[8:9, :]
    top = jnp.where(second, other[...], mine[...])
    low = jnp.where(second, mine[...], other[...])
    largest, _ = joined(
        gram,
        jnp.where(lead, own_gram[...], partner_gram[...]),
        jnp.concatenate([top, low], axis=0),
        jnp.where(lead, partner_gram[...], own_gram[...]),
    )
    finish_pair(lead, core, keys, front, back, None, largest, out, merged, gram, work)


PAIRS = ((0, 1), (2, 3), (0, 2), (0, 3), (1, 2), (1, 3))


def cross_kernel(panels, out):
    rows = panels.shape[1] - K // 2 - 8
    for at, (i, j) in enumerate(PAIRS):
        out[K * at : K * (at + 1), :] = tn(panels[i, :rows, :], panels[j, :rows, :])


def quad_kernel(last, core, mine, other, panels, *refs):
    out, (gram_a, gram_b, work_a, work_b) = refs[0], refs[-4:]
    half = K // 2
    shares = 3 * K
    rows = panels.shape[1] - half - 8
    second = core[:1, :] > 0.5

    def gram_of(i):
        own = panels[i, rows : rows + half, :]
        got = other[shares + half * i : shares + half * (i + 1), :]
        return jnp.concatenate(
            [jnp.where(second, got, own), jnp.where(second, own, got)], axis=0
        )

    def cross_of(pair):
        at = PAIRS.index(pair)
        share, lane = divmod(at, 3)
        span = slice(lane * K, lane * K + K)
        if share == 0:
            return jnp.where(second, other[span, :], mine[span, :])
        return jnp.where(second, mine[span, :], other[span, :])

    def key_of(i):
        return panels[i, rows + half : rows + half + 1, :]

    def ordered(lead, first_gram, cross, second_gram, gram):
        return joined(
            gram,
            jnp.where(lead, first_gram, second_gram),
            jnp.where(lead, cross, cross.T),
            jnp.where(lead, second_gram, first_gram),
        )

    def parted(lead, rotation):
        left, right = rotation[:, :K], rotation[:, K:]
        return jnp.where(lead, left, right), jnp.where(lead, right, left)

    lead_a, lead_b = key_of(0) < key_of(1), key_of(2) < key_of(3)
    largest_a, _ = ordered(lead_a, gram_of(0), cross_of((0, 1)), gram_of(1), gram_a)
    largest_b, _ = ordered(lead_b, gram_of(2), cross_of((2, 3)), gram_of(3), gram_b)
    prepared(gram_a, work_a, False)
    prepared(gram_b, work_b, False)
    eliminate(work_a, work_b)
    rotation_a, rotation_b = work_a[:, K:], work_b[:, K:]
    merged_a = nt(nn(rotation_a, gram_a[...]), rotation_a) * largest_a
    merged_b = nt(nn(rotation_b, gram_b[...]), rotation_b) * largest_b
    part_0, part_1 = parted(lead_a, rotation_a)
    part_2, part_3 = parted(lead_b, rotation_b)
    mixed_2 = nn(part_0, cross_of((0, 2))) + nn(part_1, cross_of((1, 2)))
    mixed_3 = nn(part_0, cross_of((0, 3))) + nn(part_1, cross_of((1, 3)))
    cross = nt(mixed_2, part_2) + nt(mixed_3, part_3)
    key_a = jnp.minimum(key_of(0), key_of(1))
    key_b = jnp.minimum(key_of(2), key_of(3))
    lead = key_a < key_b
    largest, scale = ordered(lead, merged_a, cross, merged_b, gram_a)
    prepared(gram_a, work_a, last)
    eliminate(work_a)
    rotation = work_a[:, K:]
    left, right = parted(lead, rotation)
    panel = nt(panels[0, :rows, :], nn(left, part_0))
    panel = panel + nt(panels[1, :rows, :], nn(left, part_1))
    panel = panel + nt(panels[2, :rows, :], nn(right, part_2))
    panel = panel + nt(panels[3, :rows, :], nn(right, part_3))
    if last:
        out[...] = panel * (math.sqrt(NPIX) * jnp.sqrt(scale))
    else:
        out[:rows, :] = panel
        fresh = nt(nn(rotation, gram_a[...]), rotation) * largest
        out[rows : rows + half, :] = jnp.where(second, fresh[half:, :], fresh[:half, :])
        out[rows + half :, :] = jnp.broadcast_to(jnp.minimum(key_a, key_b), (8, K))


def swapped(block, axis, bit):
    count = lax.axis_size(axis)
    return lax.ppermute(block, axis, [(low, low ^ 1 << bit) for low in range(count)])


def spread(block):
    many = jnp.broadcast_to(block[None], (PIX,) + block.shape)
    return lax.all_to_all(many, "pix", 0, 0)


def per_device(spectra, sketch, block_mask, rank_key):
    batch, width = spectra.shape
    share = batch // PIX
    rows = width // 2
    half = K // 2
    second = lax.axis_index("gal") % 2 == 1
    core_rows = jnp.broadcast_to(second.astype(jnp.float32), (8, K))
    pixel_mask = jnp.repeat(block_mask[0], width // block_mask.shape[1]).astype(jnp.bfloat16)
    masked = spectra * pixel_mask[None, :]
    sketched = lax.dot_general(
        masked, sketch, (((0,), (0,)), ((), ())), preferred_element_type=jnp.float32
    )
    sketch_gram = tn(sketched, sketched)
    key_rows = jnp.broadcast_to(rank_key.astype(jnp.float32)[:, None], (8, K))
    kept = jnp.where(second, sketched[rows:], sketched[:rows])
    sent = jnp.where(second, sketched[:rows], sketched[rows:])
    got = swapped(jnp.concatenate([sent, key_rows], axis=0), "gal", 0)
    high = lax.reduce_precision(sketched, 8, 7)
    low = sketched - high
    pieces = jnp.concatenate([high.astype(jnp.bfloat16), low.astype(jnp.bfloat16)], axis=1)
    both = jnp.dot(masked, pieces, preferred_element_type=jnp.float32)
    projected = both[:, :K] + both[:, K:]
    lead = key_rows[:1] < got[rows : rows + 1]
    front = jnp.where(lead, kept, got[:rows])
    back = jnp.where(lead, got[:rows], kept)
    sends = jnp.concatenate(
        [
            projected.reshape(PIX, share, K),
            sketch_gram.reshape(PIX, K // PIX, K),
            tn(front, back).reshape(PIX, K // PIX, K),
        ],
        axis=1,
    )
    parts = spread(jnp.sum(lax.all_to_all(sends, "pix", 0, 0), axis=0))
    own = pl.pallas_call(
        leaf_kernel,
        out_shape=jax.ShapeDtypeStruct((3 * K, K), jnp.float32),
        scratch_shapes=[pltpu.VMEM((K, 2 * K), jnp.float32), pltpu.VMEM((K, K), jnp.float32)],
        compiler_params=PARAMS,
        name="leaf",
    )(parts)
    pair_out = [
        jax.ShapeDtypeStruct((rows + half + 8, K), jnp.float32),
        jax.ShapeDtypeStruct((K, K), jnp.float32),
    ]
    pair_scratch = [
        pltpu.VMEM((2 * K, 2 * K), jnp.float32),
        pltpu.VMEM((K, 3 * K), jnp.float32),
    ]
    state, own_gram = pl.pallas_call(
        first_kernel,
        out_shape=pair_out,
        scratch_shapes=pair_scratch,
        compiler_params=PARAMS,
        name="first",
    )(
        core_rows,
        jnp.concatenate([key_rows, got[rows:]], axis=0),
        own,
        swapped(own, "gal", 0),
        front,
        back,
    )
    got = swapped(state, "gal", 1)
    kept, key_rows = state[:rows], state[rows + half :]
    lead = key_rows[:1] < got[rows + half : rows + half + 1]
    front = jnp.where(lead, kept, got[:rows])
    back = jnp.where(lead, got[:rows], kept)
    cross = tn(front, back)
    cross_sent = jnp.where(second, cross[:half], cross[half:])
    cross_kept = jnp.where(second, cross[half:], cross[:half])
    mine = jnp.sum(spread(cross_kept + swapped(cross_sent, "gal", 0)), axis=0)
    gram_half = got[rows : rows + half]
    other = swapped(jnp.concatenate([mine, gram_half], axis=0), "gal", 0)
    partner_gram = jnp.concatenate(
        [
            jnp.where(second, other[half:], gram_half),
            jnp.where(second, gram_half, other[half:]),
        ],
        axis=0,
    )
    state, own_gram = pl.pallas_call(
        merge_kernel,
        out_shape=pair_out,
        scratch_shapes=pair_scratch,
        compiler_params=PARAMS,
        name="merge",
    )(
        core_rows,
        jnp.concatenate([key_rows, got[rows + half :]], axis=0),
        mine,
        other[:half],
        own_gram,
        partner_gram,
        front,
        back,
    )
    count = lax.axis_size("gal")
    for level in (2, 4):
        last = level == 4
        if last:
            groups = [
                [base + (part << level) for part in range(4)]
                for base in range(count)
                if not base >> level & 3
            ]
            sends = jnp.broadcast_to(state[None], (4,) + state.shape)
            panels = lax.all_to_all(sends, "gal", 0, 0, axis_index_groups=groups)
        else:
            near = [state] + [
                lax.ppermute(state, "gal", [(at, at ^ part << level) for at in range(count)])
                for part in (1, 2, 3)
            ]
            place = lax.axis_index("gal") >> level
            odd, high = place % 2 == 1, place // 2 % 2 == 1
            near = [jnp.where(odd, near[part ^ 1], near[part]) for part in range(4)]
            panels = jnp.stack([jnp.where(high, near[part ^ 2], near[part]) for part in range(4)])
        cross = pl.pallas_call(
            cross_kernel,
            out_shape=jax.ShapeDtypeStruct((len(PAIRS) * K, K), jnp.float32),
            compiler_params=PARAMS,
            name="cross",
        )(panels)
        cross_sent = jnp.where(second, cross[: 3 * K], cross[3 * K :])
        cross_kept = jnp.where(second, cross[3 * K :], cross[: 3 * K])
        cross = cross_kept + swapped(cross_sent, "gal", 0)
        own = jnp.sum(lax.all_to_all(cross.reshape(PIX, -1, K), "pix", 0, 0), axis=0)
        mine = spread(own).reshape(3 * K, K)
        halves = panels[:, rows : rows + half].reshape(4 * half, K)
        other = swapped(jnp.concatenate([mine, halves], axis=0), "gal", 0)
        state = pl.pallas_call(
            functools.partial(quad_kernel, last),
            out_shape=jax.ShapeDtypeStruct((rows if last else rows + half + 8, K), jnp.float32),
            scratch_shapes=pair_scratch[:1] * 2 + pair_scratch[1:] * 2,
            compiler_params=PARAMS,
            name="finish" if last else "quad",
        )(core_rows, mine, other, panels)
    other = swapped(state, "gal", 0)
    basis = jnp.concatenate(
        [jnp.where(second, other, state), jnp.where(second, state, other)], axis=0
    )
    score_terms = jnp.dot(masked, basis.astype(jnp.bfloat16), preferred_element_type=jnp.float32)
    own_scores = jnp.sum(
        lax.all_to_all(score_terms.reshape(PIX, share, K), "pix", 0, 0), axis=0
    )
    scores = spread(own_scores * (1.0 / NPIX)).reshape(batch, K)
    return (basis, scores)


def solution(mesh):
    in_specs = (P("gal", "pix"), P("gal", None), P("gal", "pix"), P("gal"))
    out_specs = (P("pix", None), P("gal", None))
    return jax.shard_map(
        per_device, mesh=mesh, in_specs=in_specs, out_specs=out_specs, check_vma=False
    )
```

```python
import functools
import math
from itertools import zip_longest

import jax
import jax.numpy as jnp
from jax import lax
from jax.experimental import pallas as pl
from jax.experimental.pallas import tpu as pltpu
from jax.sharding import PartitionSpec as P

NPIX = 8192
K = 128
PIX = 8
HIGH = lax.Precision.HIGHEST
PARAMS = pltpu.CompilerParams(vmem_limit_bytes=32 * 1024 * 1024)
NB = 32
LANES = 128


def dot_of(a, b, dims):
    return lax.dot_general(
        a, b, (dims, ((), ())), precision=HIGH, preferred_element_type=jnp.float32
    )


def nn(a, b):
    return dot_of(a, b, ((1,), (0,)))


def nt(a, b):
    return dot_of(a, b, ((1,), (1,)))


def tn(a, b):
    return dot_of(a, b, ((0,), (0,)))


def split2(x):
    high = x.astype(jnp.bfloat16)
    return high, (x - high.astype(jnp.float32)).astype(jnp.bfloat16)


def tall(panel, factor, turned):
    dims = (((1,), (1 if turned else 0,)), ((), ()))
    high, low = split2(panel)
    factor_high, factor_low = split2(factor)

    def one(a, b):
        return lax.dot_general(a, b, dims, preferred_element_type=jnp.float32)

    return one(high, factor_high) + (one(high, factor_low) + one(low, factor_high))


def split3(x):
    high = x.astype(jnp.bfloat16)
    rest = x - high.astype(jnp.float32)
    middle = rest.astype(jnp.bfloat16)
    low = (rest - middle.astype(jnp.float32)).astype(jnp.bfloat16)
    return high, middle, low


def tn_thin(a, b):
    ah, am, al = split3(a)
    bh, bm, bl = split3(b)
    left = jnp.concatenate([ah, ah, am, am, ah, al], axis=0)
    right = jnp.concatenate([bh, bm, bh, bm, bl, bh], axis=0)
    return lax.dot_general(
        left, right, (((0,), (0,)), ((), ())), preferred_element_type=jnp.float32
    )


def whole(x):
    return jnp.broadcast_to(x, (8, LANES))


def across(x, width):
    return jnp.concatenate([x] * (width // LANES), axis=1)


def eliminate_rows(work, at):
    width = work.shape[1]
    end = (at // NB + 1) * NB
    count = (end - at) // 8 - 1
    sub = lax.broadcasted_iota(jnp.int32, (8, width), 0)
    pivots = [jnp.broadcast_to(work[at + i : at + i + 1, :K], (8, K)) for i in range(8)]
    block = [[whole(pivots[i][:, at + k : at + k + 1]) for k in range(i + 1)] for i in range(8)]
    columns = None
    if count:
        columns = [
            jnp.broadcast_to(work[at + 8 : end, at + k : at + k + 1], (8 * count, LANES)).reshape(
                count, 8, LANES
            )
            for k in range(8)
        ]
    lower, scaled_rows, multipliers = [], [], []
    result = None
    for j in range(8):
        inverse = lax.rsqrt(block[j][j])
        factors = [block[i][j] * inverse if i > j else None for i in range(8)]
        for k in range(j + 1, 8):
            for i in range(k, 8):
                block[i][k] = block[i][k] - factors[i] * factors[k]
        if count:
            multiplier = columns[j] * inverse[None]
            for k in range(j + 1, 8):
                columns[k] = columns[k] - multiplier * factors[k][None]
            multipliers.append(multiplier)
        row = jnp.broadcast_to(work[at + j : at + j + 1, :], (8, width))
        for q in range(j):
            row = row - across(lower[q][j], width) * scaled_rows[q]
        row = row * across(inverse, width)
        lower.append(factors)
        scaled_rows.append(row)
        result = row if result is None else jnp.where(sub >= j, row, result)
        yield
    work[at : at + 8, :] = result
    for t in range(count):
        rows = work[at + 8 + 8 * t : at + 16 + 8 * t, :]
        for j in range(8):
            rows = rows - across(multipliers[j][t], width) * scaled_rows[j]
        work[at + 8 + 8 * t : at + 16 + 8 * t, :] = rows
        yield
    if at + 8 == end and end < K:
        group = work[end - NB : end, :]
        work[end:, :] = work[end:, :] - tn_thin(group[:, end:K], group)


def eliminate(*works):
    for at in range(0, K, 8):
        for _ in zip_longest(*[eliminate_rows(work, at) for work in works]):
            pass


def leaf_kernel(parts, out, work_z, work_h):
    share = parts.shape[1] - 2 * K // PIX
    step = K // PIX
    summed = parts[:, :share, :].reshape(PIX * share, K)
    work_h[...] = tn(summed, summed)
    for part in range(PIX):
        span = slice(step * part, step * (part + 1))
        work_z[span, :K] = parts[part, share : share + step, :]
        out[2 * K + step * part : 2 * K + step * (part + 1), :] = parts[part, share + step :, :]
    row_at = lax.broadcasted_iota(jnp.int32, (K, K), 0)
    col_at = lax.broadcasted_iota(jnp.int32, (K, K), 1)
    work_z[:, K:] = jnp.where(row_at == col_at, 1.0, 0.0)
    eliminate(work_z, work_h)
    inverse = work_z[:, K:]
    factor = nt(inverse, jnp.where(col_at >= row_at, work_h[...], 0.0))
    out[:K, :] = tn(inverse, factor)
    out[K : 2 * K, :] = tn(factor, factor)


def joined(gram, front_gram, cross, back_gram):
    largest = jnp.maximum(
        jnp.max(front_gram, keepdims=True), jnp.max(back_gram, keepdims=True)
    )
    scale = 1.0 / largest
    gram[:K, :K] = front_gram * scale
    gram[:K, K:] = cross * scale
    gram[K:, :K] = cross.T * scale
    gram[K:, K:] = back_gram * scale
    return largest, scale


def prepared(gram, work, last):
    powered = nn(gram[:K, :], gram[...])
    if last:
        work[:, :K] = nt(nn(powered, gram[...]), powered)
    else:
        work[:, :K] = nt(powered, powered)
    work[:, K:] = powered


def finish_pair(lead, core, keys, front, back, coefficients, largest, out, merged, gram, work):
    rows = front.shape[0]
    half = K // 2
    second = core[:1, :] > 0.5
    prepared(gram, work, False)
    eliminate(work)
    rotation = work[:, K:]
    if coefficients is None:
        out[:rows, :] = tall(front[...], rotation[:, :K], True) + tall(
            back[...], rotation[:, K:], True
        )
    else:
        left, right = coefficients
        out[:rows, :] = tall(front[...], nt(left, rotation[:, :K]), False) + tall(
            back[...], nt(right, rotation[:, K:]), False
        )
    fresh = nt(nn(rotation, gram[...]), rotation) * largest
    merged[...] = fresh
    out[rows : rows + half, :] = jnp.where(second, fresh[half:, :], fresh[:half, :])
    out[rows + half :, :] = jnp.minimum(keys[:8, :], keys[8:, :])


def first_kernel(core, keys, own, other, front, back, out, merged, gram, work):
    lead = keys[:1, :] < keys[8:9, :]
    left = jnp.where(lead, own[:K, :], other[:K, :])
    right = jnp.where(lead, other[:K, :], own[:K, :])
    cross = own[2 * K :, :] + other[2 * K :, :]
    largest, _ = joined(
        gram,
        jnp.where(lead, own[K : 2 * K, :], other[K : 2 * K, :]),
        nn(tn(left, cross), right),
        jnp.where(lead, other[K : 2 * K, :], own[K : 2 * K, :]),
    )
    finish_pair(lead, core, keys, front, back, (left, right), largest, out, merged, gram, work)


def merge_kernel(core, keys, mine, other, own_gram, partner_gram, front, back, *refs):
    out, merged, gram, work = refs
    second = core[:1, :] > 0.5
    lead = keys[:1, :] < keys[8:9, :]
    top = jnp.where(second, other[...], mine[...])
    low = jnp.where(second, mine[...], other[...])
    largest, _ = joined(
        gram,
        jnp.where(lead, own_gram[...], partner_gram[...]),
        jnp.concatenate([top, low], axis=0),
        jnp.where(lead, partner_gram[...], own_gram[...]),
    )
    finish_pair(lead, core, keys, front, back, None, largest, out, merged, gram, work)


PAIRS = ((0, 1), (2, 3), (0, 2), (0, 3), (1, 2), (1, 3))


def cross_kernel(panels, out):
    rows = panels.shape[1] - K // 2 - 8
    for at, (i, j) in enumerate(PAIRS):
        out[K * at : K * (at + 1), :] = tn(panels[i, :rows, :], panels[j, :rows, :])


def quad_kernel(last, core, mine, other, panels, *refs):
    out, (gram_a, gram_b, work_a, work_b) = refs[0], refs[-4:]
    half = K // 2
    shares = 3 * K
    rows = panels.shape[1] - half - 8
    second = core[:1, :] > 0.5

    def gram_of(i):
        own = panels[i, rows : rows + half, :]
        got = other[shares + half * i : shares + half * (i + 1), :]
        return jnp.concatenate(
            [jnp.where(second, got, own), jnp.where(second, own, got)], axis=0
        )

    def cross_of(pair):
        at = PAIRS.index(pair)
        share, lane = divmod(at, 3)
        span = slice(lane * K, lane * K + K)
        if share == 0:
            return jnp.where(second, other[span, :], mine[span, :])
        return jnp.where(second, mine[span, :], other[span, :])

    def key_of(i):
        return panels[i, rows + half : rows + half + 1, :]

    def ordered(lead, first_gram, cross, second_gram, gram):
        return joined(
            gram,
            jnp.where(lead, first_gram, second_gram),
            jnp.where(lead, cross, cross.T),
            jnp.where(lead, second_gram, first_gram),
        )

    def parted(lead, rotation):
        left, right = rotation[:, :K], rotation[:, K:]
        return jnp.where(lead, left, right), jnp.where(lead, right, left)

    lead_a, lead_b = key_of(0) < key_of(1), key_of(2) < key_of(3)
    largest_a, _ = ordered(lead_a, gram_of(0), cross_of((0, 1)), gram_of(1), gram_a)
    largest_b, _ = ordered(lead_b, gram_of(2), cross_of((2, 3)), gram_of(3), gram_b)
    prepared(gram_a, work_a, False)
    prepared(gram_b, work_b, False)
    eliminate(work_a, work_b)
    rotation_a, rotation_b = work_a[:, K:], work_b[:, K:]
    merged_a = nt(nn(rotation_a, gram_a[...]), rotation_a) * largest_a
    merged_b = nt(nn(rotation_b, gram_b[...]), rotation_b) * largest_b
    part_0, part_1 = parted(lead_a, rotation_a)
    part_2, part_3 = parted(lead_b, rotation_b)
    mixed_2 = nn(part_0, cross_of((0, 2))) + nn(part_1, cross_of((1, 2)))
    mixed_3 = nn(part_0, cross_of((0, 3))) + nn(part_1, cross_of((1, 3)))
    cross = nt(mixed_2, part_2) + nt(mixed_3, part_3)
    key_a = jnp.minimum(key_of(0), key_of(1))
    key_b = jnp.minimum(key_of(2), key_of(3))
    lead = key_a < key_b
    largest, scale = ordered(lead, merged_a, cross, merged_b, gram_a)
    prepared(gram_a, work_a, last)
    eliminate(work_a)
    rotation = work_a[:, K:]
    left, right = parted(lead, rotation)
    panel = tall(panels[0, :rows, :], nn(left, part_0), True)
    panel = panel + tall(panels[1, :rows, :], nn(left, part_1), True)
    panel = panel + tall(panels[2, :rows, :], nn(right, part_2), True)
    panel = panel + tall(panels[3, :rows, :], nn(right, part_3), True)
    if last:
        out[...] = panel * (math.sqrt(NPIX) * jnp.sqrt(scale))
    else:
        out[:rows, :] = panel
        fresh = nt(nn(rotation, gram_a[...]), rotation) * largest
        out[rows : rows + half, :] = jnp.where(second, fresh[half:, :], fresh[:half, :])
        out[rows + half :, :] = jnp.broadcast_to(jnp.minimum(key_a, key_b), (8, K))


def swapped(block, axis, bit):
    count = lax.axis_size(axis)
    return lax.ppermute(block, axis, [(low, low ^ 1 << bit) for low in range(count)])


def spread(block):
    many = jnp.broadcast_to(block[None], (PIX,) + block.shape)
    return lax.all_to_all(many, "pix", 0, 0)


def per_device(spectra, sketch, block_mask, rank_key):
    batch, width = spectra.shape
    share = batch // PIX
    rows = width // 2
    half = K // 2
    second = lax.axis_index("gal") % 2 == 1
    core_rows = jnp.broadcast_to(second.astype(jnp.float32), (8, K))
    pixel_mask = jnp.repeat(block_mask[0], width // block_mask.shape[1]).astype(jnp.bfloat16)
    masked = spectra * pixel_mask[None, :]
    sketched = lax.dot_general(
        masked, sketch, (((0,), (0,)), ((), ())), preferred_element_type=jnp.float32
    )
    sketch_gram = tn(sketched, sketched)
    key_rows = jnp.broadcast_to(rank_key.astype(jnp.float32)[:, None], (8, K))
    kept = jnp.where(second, sketched[rows:], sketched[:rows])
    sent = jnp.where(second, sketched[:rows], sketched[rows:])
    got = swapped(jnp.concatenate([sent, key_rows], axis=0), "gal", 0)
    high = lax.reduce_precision(sketched, 8, 7)
    low = sketched - high
    pieces = jnp.concatenate([high.astype(jnp.bfloat16), low.astype(jnp.bfloat16)], axis=1)
    both = jnp.dot(masked, pieces, preferred_element_type=jnp.float32)
    projected = both[:, :K] + both[:, K:]
    lead = key_rows[:1] < got[rows : rows + 1]
    front = jnp.where(lead, kept, got[:rows])
    back = jnp.where(lead, got[:rows], kept)
    sends = jnp.concatenate(
        [
            projected.reshape(PIX, share, K),
            sketch_gram.reshape(PIX, K // PIX, K),
            tn(front, back).reshape(PIX, K // PIX, K),
        ],
        axis=1,
    )
    parts = spread(jnp.sum(lax.all_to_all(sends, "pix", 0, 0), axis=0))
    own = pl.pallas_call(
        leaf_kernel,
        out_shape=jax.ShapeDtypeStruct((3 * K, K), jnp.float32),
        scratch_shapes=[pltpu.VMEM((K, 2 * K), jnp.float32), pltpu.VMEM((K, K), jnp.float32)],
        compiler_params=PARAMS,
        name="leaf",
    )(parts)
    pair_out = [
        jax.ShapeDtypeStruct((rows + half + 8, K), jnp.float32),
        jax.ShapeDtypeStruct((K, K), jnp.float32),
    ]
    pair_scratch = [
        pltpu.VMEM((2 * K, 2 * K), jnp.float32),
        pltpu.VMEM((K, 3 * K), jnp.float32),
    ]
    state, own_gram = pl.pallas_call(
        first_kernel,
        out_shape=pair_out,
        scratch_shapes=pair_scratch,
        compiler_params=PARAMS,
        name="first",
    )(
        core_rows,
        jnp.concatenate([key_rows, got[rows:]], axis=0),
        own,
        swapped(own, "gal", 0),
        front,
        back,
    )
    got = swapped(state, "gal", 1)
    kept, key_rows = state[:rows], state[rows + half :]
    lead = key_rows[:1] < got[rows + half : rows + half + 1]
    front = jnp.where(lead, kept, got[:rows])
    back = jnp.where(lead, got[:rows], kept)
    cross = tn(front, back)
    cross_sent = jnp.where(second, cross[:half], cross[half:])
    cross_kept = jnp.where(second, cross[half:], cross[:half])
    cross = cross_kept + swapped(cross_sent, "gal", 0)
    pair_keys = jnp.concatenate([key_rows, got[rows + half :]], axis=0)
    cross, gram_half, pair_keys = lax.optimization_barrier(
        (cross, got[rows : rows + half], pair_keys)
    )
    mine = jnp.sum(spread(cross), axis=0)
    other = swapped(jnp.concatenate([mine, gram_half], axis=0), "gal", 0)
    partner_gram = jnp.concatenate(
        [
            jnp.where(second, other[half:], gram_half),
            jnp.where(second, gram_half, other[half:]),
        ],
        axis=0,
    )
    state, own_gram = pl.pallas_call(
        merge_kernel,
        out_shape=pair_out,
        scratch_shapes=pair_scratch,
        compiler_params=PARAMS,
        name="merge",
    )(
        core_rows,
        pair_keys,
        mine,
        other[:half],
        own_gram,
        partner_gram,
        front,
        back,
    )
    count = lax.axis_size("gal")
    for level in (2, 4):
        last = level == 4
        if last:
            groups = [
                [base + (part << level) for part in range(4)]
                for base in range(count)
                if not base >> level & 3
            ]
            sends = jnp.broadcast_to(state[None], (4,) + state.shape)
            panels = lax.all_to_all(sends, "gal", 0, 0, axis_index_groups=groups)
        else:
            near = [state] + [
                lax.ppermute(state, "gal", [(at, at ^ part << level) for at in range(count)])
                for part in (1, 2, 3)
            ]
            place = lax.axis_index("gal") >> level
            odd, high = place % 2 == 1, place // 2 % 2 == 1
            near = [jnp.where(odd, near[part ^ 1], near[part]) for part in range(4)]
            panels = jnp.stack([jnp.where(high, near[part ^ 2], near[part]) for part in range(4)])
        cross = pl.pallas_call(
            cross_kernel,
            out_shape=jax.ShapeDtypeStruct((len(PAIRS) * K, K), jnp.float32),
            compiler_params=PARAMS,
            name="cross",
        )(panels)
        cross_sent = jnp.where(second, cross[: 3 * K], cross[3 * K :])
        cross_kept = jnp.where(second, cross[3 * K :], cross[: 3 * K])
        cross = cross_kept + swapped(cross_sent, "gal", 0)
        halves = panels[:, rows : rows + half].reshape(4 * half, K)
        cross, halves = lax.optimization_barrier((cross, halves))
        own = jnp.sum(lax.all_to_all(cross.reshape(PIX, -1, K), "pix", 0, 0), axis=0)
        mine = spread(own).reshape(3 * K, K)
        other = swapped(jnp.concatenate([mine, halves], axis=0), "gal", 0)
        state = pl.pallas_call(
            functools.partial(quad_kernel, last),
            out_shape=jax.ShapeDtypeStruct((rows if last else rows + half + 8, K), jnp.float32),
            scratch_shapes=pair_scratch[:1] * 2 + pair_scratch[1:] * 2,
            compiler_params=PARAMS,
            name="finish" if last else "quad",
        )(core_rows, mine, other, panels)
    other = swapped(state, "gal", 0)
    basis = jnp.concatenate(
        [jnp.where(second, other, state), jnp.where(second, state, other)], axis=0
    )
    score_terms = jnp.dot(masked, basis.astype(jnp.bfloat16), preferred_element_type=jnp.float32)
    own_scores = jnp.sum(
        lax.all_to_all(score_terms.reshape(PIX, share, K), "pix", 0, 0), axis=0
    )
    scores = spread(own_scores * (1.0 / NPIX)).reshape(batch, K)
    return (basis, scores)


def solution(mesh):
    in_specs = (P("gal", "pix"), P("gal", None), P("gal", "pix"), P("gal"))
    out_specs = (P("pix", None), P("gal", None))
    return jax.shard_map(
        per_device, mesh=mesh, in_specs=in_specs, out_specs=out_specs, check_vma=False
    )
```

```python
import functools
import math
from itertools import zip_longest

import jax
import jax.numpy as jnp
from jax import lax
from jax.experimental import pallas as pl
from jax.experimental.pallas import tpu as pltpu
from jax.sharding import PartitionSpec as P

NPIX = 8192
K = 128
PIX = 8
HIGH = lax.Precision.HIGHEST
PARAMS = pltpu.CompilerParams(vmem_limit_bytes=32 * 1024 * 1024)
NB = 32
LANES = 128


def dot_of(a, b, dims):
    return lax.dot_general(
        a, b, (dims, ((), ())), precision=HIGH, preferred_element_type=jnp.float32
    )


def nn(a, b):
    return dot_of(a, b, ((1,), (0,)))


def nt(a, b):
    return dot_of(a, b, ((1,), (1,)))


def tn(a, b):
    return dot_of(a, b, ((0,), (0,)))


def split2(x):
    high = x.astype(jnp.bfloat16)
    return high, (x - high.astype(jnp.float32)).astype(jnp.bfloat16)


def tall(panel, factor, turned):
    dims = (((1,), (1 if turned else 0,)), ((), ()))
    high, low = split2(panel)
    factor_high, factor_low = split2(factor)

    def one(a, b):
        return lax.dot_general(a, b, dims, preferred_element_type=jnp.float32)

    return one(high, factor_high) + (one(high, factor_low) + one(low, factor_high))


def split3(x):
    high = x.astype(jnp.bfloat16)
    rest = x - high.astype(jnp.float32)
    middle = rest.astype(jnp.bfloat16)
    low = (rest - middle.astype(jnp.float32)).astype(jnp.bfloat16)
    return high, middle, low


def tn_thin(a, b):
    ah, am, al = split3(a)
    bh, bm, bl = split3(b)
    left = jnp.concatenate([ah, ah, am, am, ah, al], axis=0)
    right = jnp.concatenate([bh, bm, bh, bm, bl, bh], axis=0)
    return lax.dot_general(
        left, right, (((0,), (0,)), ((), ())), preferred_element_type=jnp.float32
    )


def whole(x):
    return jnp.broadcast_to(x, (8, LANES))


def across(x, width):
    return jnp.concatenate([x] * (width // LANES), axis=1)


def eliminate_rows(work, at):
    width = work.shape[1]
    end = (at // NB + 1) * NB
    count = (end - at) // 8 - 1
    sub = lax.broadcasted_iota(jnp.int32, (8, width), 0)
    pivots = [jnp.broadcast_to(work[at + i : at + i + 1, :K], (8, K)) for i in range(8)]
    block = [[whole(pivots[i][:, at + k : at + k + 1]) for k in range(i + 1)] for i in range(8)]
    columns = None
    if count:
        columns = [
            jnp.broadcast_to(work[at + 8 : end, at + k : at + k + 1], (8 * count, LANES)).reshape(
                count, 8, LANES
            )
            for k in range(8)
        ]
    lower, scaled_rows, multipliers = [], [], []
    result = None
    for j in range(8):
        inverse = lax.rsqrt(block[j][j])
        factors = [block[i][j] * inverse if i > j else None for i in range(8)]
        for k in range(j + 1, 8):
            for i in range(k, 8):
                block[i][k] = block[i][k] - factors[i] * factors[k]
        if count:
            multiplier = columns[j] * inverse[None]
            for k in range(j + 1, 8):
                columns[k] = columns[k] - multiplier * factors[k][None]
            multipliers.append(multiplier)
        row = jnp.broadcast_to(work[at + j : at + j + 1, :], (8, width))
        for q in range(j):
            row = row - across(lower[q][j], width) * scaled_rows[q]
        row = row * across(inverse, width)
        lower.append(factors)
        scaled_rows.append(row)
        result = row if result is None else jnp.where(sub >= j, row, result)
        yield
    work[at : at + 8, :] = result
    for t in range(count):
        rows = work[at + 8 + 8 * t : at + 16 + 8 * t, :]
        for j in range(8):
            rows = rows - across(multipliers[j][t], width) * scaled_rows[j]
        work[at + 8 + 8 * t : at + 16 + 8 * t, :] = rows
        yield
    if at + 8 == end and end < K:
        group = work[end - NB : end, :]
        work[end:, :] = work[end:, :] - tn_thin(group[:, end:K], group)


def eliminate(*works):
    for at in range(0, K, 8):
        for _ in zip_longest(*[eliminate_rows(work, at) for work in works]):
            pass


def leaf_kernel(parts, out, work_z, work_h):
    share = parts.shape[1] - 2 * K // PIX
    step = K // PIX
    summed = parts[:, :share, :].reshape(PIX * share, K)
    work_h[...] = tn(summed, summed)
    for part in range(PIX):
        span = slice(step * part, step * (part + 1))
        work_z[span, :K] = parts[part, share : share + step, :]
        out[2 * K + step * part : 2 * K + step * (part + 1), :] = parts[part, share + step :, :]
    row_at = lax.broadcasted_iota(jnp.int32, (K, K), 0)
    col_at = lax.broadcasted_iota(jnp.int32, (K, K), 1)
    work_z[:, K:] = jnp.where(row_at == col_at, 1.0, 0.0)
    eliminate(work_z, work_h)
    inverse = work_z[:, K:]
    factor = nt(inverse, jnp.where(col_at >= row_at, work_h[...], 0.0))
    out[:K, :] = tn(inverse, factor)
    out[K : 2 * K, :] = tn(factor, factor)


def joined(gram, front_gram, cross, back_gram):
    largest = jnp.maximum(
        jnp.max(front_gram, keepdims=True), jnp.max(back_gram, keepdims=True)
    )
    scale = 1.0 / largest
    gram[:K, :K] = front_gram * scale
    gram[:K, K:] = cross * scale
    gram[K:, :K] = cross.T * scale
    gram[K:, K:] = back_gram * scale
    return largest, scale


def prepared(gram, work, last):
    powered = nn(gram[:K, :], gram[...])
    if last:
        work[:, :K] = nt(nn(powered, gram[...]), powered)
    else:
        work[:, :K] = nt(powered, powered)
    work[:, K:] = powered


def finish_pair(lead, core, keys, front, back, coefficients, largest, out, merged, gram, work):
    rows = front.shape[0]
    half = K // 2
    second = core[:1, :] > 0.5
    prepared(gram, work, False)
    eliminate(work)
    rotation = work[:, K:]
    if coefficients is None:
        out[:rows, :] = tall(front[...], rotation[:, :K], True) + tall(
            back[...], rotation[:, K:], True
        )
    else:
        left, right = coefficients
        out[:rows, :] = tall(front[...], nt(left, rotation[:, :K]), False) + tall(
            back[...], nt(right, rotation[:, K:]), False
        )
    fresh = nt(nn(rotation, gram[...]), rotation) * largest
    merged[...] = fresh
    out[rows : rows + half, :] = jnp.where(second, fresh[half:, :], fresh[:half, :])
    out[rows + half :, :] = jnp.minimum(keys[:8, :], keys[8:, :])


def first_kernel(core, keys, own, other, front, back, out, merged, gram, work):
    lead = keys[:1, :] < keys[8:9, :]
    left = jnp.where(lead, own[:K, :], other[:K, :])
    right = jnp.where(lead, other[:K, :], own[:K, :])
    cross = own[2 * K :, :] + other[2 * K :, :]
    largest, _ = joined(
        gram,
        jnp.where(lead, own[K : 2 * K, :], other[K : 2 * K, :]),
        nn(tn(left, cross), right),
        jnp.where(lead, other[K : 2 * K, :], own[K : 2 * K, :]),
    )
    finish_pair(lead, core, keys, front, back, (left, right), largest, out, merged, gram, work)


def merge_kernel(core, keys, mine, other, own_gram, partner_gram, front, back, *refs):
    out, merged, gram, work = refs
    second = core[:1, :] > 0.5
    lead = keys[:1, :] < keys[8:9, :]
    top = jnp.where(second, other[...], mine[...])
    low = jnp.where(second, mine[...], other[...])
    largest, _ = joined(
        gram,
        jnp.where(lead, own_gram[...], partner_gram[...]),
        jnp.concatenate([top, low], axis=0),
        jnp.where(lead, partner_gram[...], own_gram[...]),
    )
    finish_pair(lead, core, keys, front, back, None, largest, out, merged, gram, work)


PAIRS = ((0, 1), (2, 3), (0, 2), (0, 3), (1, 2), (1, 3))


def cross_kernel(panels, out):
    rows = panels.shape[1] - K // 2 - 8
    for at, (i, j) in enumerate(PAIRS):
        out[K * at : K * (at + 1), :] = tn(panels[i, :rows, :], panels[j, :rows, :])


def quad_kernel(last, core, mine, other, panels, *refs):
    out, (gram_a, gram_b, work_a, work_b) = refs[0], refs[-4:]
    half = K // 2
    shares = 3 * K
    rows = panels.shape[1] - half - 8
    second = core[:1, :] > 0.5

    def gram_of(i):
        own = panels[i, rows : rows + half, :]
        got = other[shares + half * i : shares + half * (i + 1), :]
        return jnp.concatenate(
            [jnp.where(second, got, own), jnp.where(second, own, got)], axis=0
        )

    def cross_of(pair):
        at = PAIRS.index(pair)
        share, lane = divmod(at, 3)
        span = slice(lane * K, lane * K + K)
        if share == 0:
            return jnp.where(second, other[span, :], mine[span, :])
        return jnp.where(second, mine[span, :], other[span, :])

    def key_of(i):
        return panels[i, rows + half : rows + half + 1, :]

    def ordered(lead, first_gram, cross, second_gram, gram):
        return joined(
            gram,
            jnp.where(lead, first_gram, second_gram),
            jnp.where(lead, cross, cross.T),
            jnp.where(lead, second_gram, first_gram),
        )

    def parted(lead, rotation):
        left, right = rotation[:, :K], rotation[:, K:]
        return jnp.where(lead, left, right), jnp.where(lead, right, left)

    lead_a, lead_b = key_of(0) < key_of(1), key_of(2) < key_of(3)
    largest_a, _ = ordered(lead_a, gram_of(0), cross_of((0, 1)), gram_of(1), gram_a)
    largest_b, _ = ordered(lead_b, gram_of(2), cross_of((2, 3)), gram_of(3), gram_b)
    prepared(gram_a, work_a, False)
    prepared(gram_b, work_b, False)
    eliminate(work_a, work_b)
    rotation_a, rotation_b = work_a[:, K:], work_b[:, K:]
    merged_a = nt(nn(rotation_a, gram_a[...]), rotation_a) * largest_a
    merged_b = nt(nn(rotation_b, gram_b[...]), rotation_b) * largest_b
    part_0, part_1 = parted(lead_a, rotation_a)
    part_2, part_3 = parted(lead_b, rotation_b)
    mixed_2 = nn(part_0, cross_of((0, 2))) + nn(part_1, cross_of((1, 2)))
    mixed_3 = nn(part_0, cross_of((0, 3))) + nn(part_1, cross_of((1, 3)))
    cross = nt(mixed_2, part_2) + nt(mixed_3, part_3)
    key_a = jnp.minimum(key_of(0), key_of(1))
    key_b = jnp.minimum(key_of(2), key_of(3))
    lead = key_a < key_b
    largest, scale = ordered(lead, merged_a, cross, merged_b, gram_a)
    prepared(gram_a, work_a, last)
    eliminate(work_a)
    rotation = work_a[:, K:]
    left, right = parted(lead, rotation)
    panel = tall(panels[0, :rows, :], nn(left, part_0), True)
    panel = panel + tall(panels[1, :rows, :], nn(left, part_1), True)
    panel = panel + tall(panels[2, :rows, :], nn(right, part_2), True)
    panel = panel + tall(panels[3, :rows, :], nn(right, part_3), True)
    if last:
        out[...] = panel * (math.sqrt(NPIX) * jnp.sqrt(scale))
    else:
        out[:rows, :] = panel
        fresh = nt(nn(rotation, gram_a[...]), rotation) * largest
        out[rows : rows + half, :] = jnp.where(second, fresh[half:, :], fresh[:half, :])
        out[rows + half :, :] = jnp.broadcast_to(jnp.minimum(key_a, key_b), (8, K))


def swapped(block, axis, bit):
    count = lax.axis_size(axis)
    return lax.ppermute(block, axis, [(low, low ^ 1 << bit) for low in range(count)])


def spread(block):
    many = jnp.broadcast_to(block[None], (PIX,) + block.shape)
    return lax.all_to_all(many, "pix", 0, 0)


def per_device(spectra, sketch, block_mask, rank_key):
    batch, width = spectra.shape
    share = batch // PIX
    rows = width // 2
    half = K // 2
    second = lax.axis_index("gal") % 2 == 1
    core_rows = jnp.broadcast_to(second.astype(jnp.float32), (8, K))
    pixel_mask = jnp.repeat(block_mask[0], width // block_mask.shape[1]).astype(jnp.bfloat16)
    masked = spectra * pixel_mask[None, :]
    sketched = lax.dot_general(
        masked, sketch, (((0,), (0,)), ((), ())), preferred_element_type=jnp.float32
    )
    sketch_gram = tn(sketched, sketched)
    key_rows = jnp.broadcast_to(rank_key.astype(jnp.float32)[:, None], (8, K))
    kept = jnp.where(second, sketched[rows:], sketched[:rows])
    sent = jnp.where(second, sketched[:rows], sketched[rows:])
    got = swapped(jnp.concatenate([sent, key_rows], axis=0), "gal", 0)
    high = lax.reduce_precision(sketched, 8, 7)
    low = sketched - high
    pieces = jnp.concatenate([high.astype(jnp.bfloat16), low.astype(jnp.bfloat16)], axis=1)
    both = jnp.dot(masked, pieces, preferred_element_type=jnp.float32)
    projected = both[:, :K] + both[:, K:]
    lead = key_rows[:1] < got[rows : rows + 1]
    front = jnp.where(lead, kept, got[:rows])
    back = jnp.where(lead, got[:rows], kept)
    sends = jnp.concatenate(
        [
            projected.reshape(PIX, share, K),
            sketch_gram.reshape(PIX, K // PIX, K),
            tn(front, back).reshape(PIX, K // PIX, K),
        ],
        axis=1,
    )
    parts = spread(jnp.sum(lax.all_to_all(sends, "pix", 0, 0), axis=0))
    own = pl.pallas_call(
        leaf_kernel,
        out_shape=jax.ShapeDtypeStruct((3 * K, K), jnp.float32),
        scratch_shapes=[pltpu.VMEM((K, 2 * K), jnp.float32), pltpu.VMEM((K, K), jnp.float32)],
        compiler_params=PARAMS,
        name="leaf",
    )(parts)
    pair_out = [
        jax.ShapeDtypeStruct((rows + half + 8, K), jnp.float32),
        jax.ShapeDtypeStruct((K, K), jnp.float32),
    ]
    pair_scratch = [
        pltpu.VMEM((2 * K, 2 * K), jnp.float32),
        pltpu.VMEM((K, 3 * K), jnp.float32),
    ]
    state, own_gram = pl.pallas_call(
        first_kernel,
        out_shape=pair_out,
        scratch_shapes=pair_scratch,
        compiler_params=PARAMS,
        name="first",
    )(
        core_rows,
        jnp.concatenate([key_rows, got[rows:]], axis=0),
        own,
        swapped(own, "gal", 0),
        front,
        back,
    )
    got = swapped(state, "gal", 1)
    kept, key_rows = state[:rows], state[rows + half :]
    lead = key_rows[:1] < got[rows + half : rows + half + 1]
    front = jnp.where(lead, kept, got[:rows])
    back = jnp.where(lead, got[:rows], kept)
    cross = tn(front, back)
    cross_sent = jnp.where(second, cross[:half], cross[half:])
    cross_kept = jnp.where(second, cross[half:], cross[:half])
    cross = cross_kept + swapped(cross_sent, "gal", 0)
    pair_keys = jnp.concatenate([key_rows, got[rows + half :]], axis=0)
    cross, gram_half, pair_keys = lax.optimization_barrier(
        (cross, got[rows : rows + half], pair_keys)
    )
    mine = jnp.sum(spread(cross), axis=0)
    other = swapped(jnp.concatenate([mine, gram_half], axis=0), "gal", 0)
    partner_gram = jnp.concatenate(
        [
            jnp.where(second, other[half:], gram_half),
            jnp.where(second, gram_half, other[half:]),
        ],
        axis=0,
    )
    state, own_gram = pl.pallas_call(
        merge_kernel,
        out_shape=pair_out,
        scratch_shapes=pair_scratch,
        compiler_params=PARAMS,
        name="merge",
    )(
        core_rows,
        pair_keys,
        mine,
        other[:half],
        own_gram,
        partner_gram,
        front,
        back,
    )
    count = lax.axis_size("gal")
    for level in (2, 4):
        last = level == 4
        if last:
            groups = [
                [base + (part << level) for part in range(4)]
                for base in range(count)
                if not base >> level & 3
            ]
            sends = jnp.broadcast_to(state[None], (4,) + state.shape)
            panels = lax.all_to_all(sends, "gal", 0, 0, axis_index_groups=groups)
        else:
            near = [state] + [
                lax.ppermute(state, "gal", [(at, at ^ step) for at in range(count)])
                for step in (1 << level, 2 << level | 2, 3 << level)
            ]
            place = lax.axis_index("gal") >> level
            odd, high = place % 2 == 1, place // 2 % 2 == 1
            near = [jnp.where(odd, near[part ^ 1], near[part]) for part in range(4)]
            panels = jnp.stack([jnp.where(high, near[part ^ 2], near[part]) for part in range(4)])
        cross = pl.pallas_call(
            cross_kernel,
            out_shape=jax.ShapeDtypeStruct((len(PAIRS) * K, K), jnp.float32),
            compiler_params=PARAMS,
            name="cross",
        )(panels)
        cross_sent = jnp.where(second, cross[: 3 * K], cross[3 * K :])
        cross_kept = jnp.where(second, cross[3 * K :], cross[: 3 * K])
        cross = cross_kept + swapped(cross_sent, "gal", 0)
        halves = panels[:, rows : rows + half].reshape(4 * half, K)
        cross, halves = lax.optimization_barrier((cross, halves))
        own = jnp.sum(lax.all_to_all(cross.reshape(PIX, -1, K), "pix", 0, 0), axis=0)
        mine = spread(own).reshape(3 * K, K)
        other = swapped(jnp.concatenate([mine, halves], axis=0), "gal", 0)
        state = pl.pallas_call(
            functools.partial(quad_kernel, last),
            out_shape=jax.ShapeDtypeStruct((rows if last else rows + half + 8, K), jnp.float32),
            scratch_shapes=pair_scratch[:1] * 2 + pair_scratch[1:] * 2,
            compiler_params=PARAMS,
            name="finish" if last else "quad",
        )(core_rows, mine, other, panels)
    other = swapped(state, "gal", 0)
    basis = jnp.concatenate(
        [jnp.where(second, other, state), jnp.where(second, state, other)], axis=0
    )
    score_terms = jnp.dot(masked, basis.astype(jnp.bfloat16), preferred_element_type=jnp.float32)
    own_scores = jnp.sum(
        lax.all_to_all(score_terms.reshape(PIX, share, K), "pix", 0, 0), axis=0
    )
    scores = spread(own_scores * (1.0 / NPIX)).reshape(batch, K)
    return (basis, scores)


def solution(mesh):
    in_specs = (P("gal", "pix"), P("gal", None), P("gal", "pix"), P("gal"))
    out_specs = (P("pix", None), P("gal", None))
    return jax.shard_map(
        per_device, mesh=mesh, in_specs=in_specs, out_specs=out_specs, check_vma=False
    )
```

```python
import functools
import math
from itertools import zip_longest

import jax
import jax.numpy as jnp
from jax import lax
from jax.experimental import pallas as pl
from jax.experimental.pallas import tpu as pltpu
from jax.sharding import PartitionSpec as P

NPIX = 8192
K = 128
PIX = 8
HIGH = lax.Precision.HIGHEST
PARAMS = pltpu.CompilerParams(vmem_limit_bytes=32 * 1024 * 1024)
NB = 32
LANES = 128


def dot_of(a, b, dims):
    return lax.dot_general(
        a, b, (dims, ((), ())), precision=HIGH, preferred_element_type=jnp.float32
    )


def nn(a, b):
    return dot_of(a, b, ((1,), (0,)))


def nt(a, b):
    return dot_of(a, b, ((1,), (1,)))


def tn(a, b):
    return dot_of(a, b, ((0,), (0,)))


def split2(x):
    high = x.astype(jnp.bfloat16)
    return high, (x - high.astype(jnp.float32)).astype(jnp.bfloat16)


def tall(panel, factor, turned):
    dims = (((1,), (1 if turned else 0,)), ((), ()))
    high, low = split2(panel)
    factor_high, factor_low = split2(factor)

    def one(a, b):
        return lax.dot_general(a, b, dims, preferred_element_type=jnp.float32)

    return one(high, factor_high) + (one(high, factor_low) + one(low, factor_high))


def split3(x):
    high = x.astype(jnp.bfloat16)
    rest = x - high.astype(jnp.float32)
    middle = rest.astype(jnp.bfloat16)
    low = (rest - middle.astype(jnp.float32)).astype(jnp.bfloat16)
    return high, middle, low


def tn_thin(a, b):
    ah, am, al = split3(a)
    bh, bm, bl = split3(b)
    left = jnp.concatenate([ah, ah, am, am, ah, al], axis=0)
    right = jnp.concatenate([bh, bm, bh, bm, bl, bh], axis=0)
    return lax.dot_general(
        left, right, (((0,), (0,)), ((), ())), preferred_element_type=jnp.float32
    )


def whole(x):
    return jnp.broadcast_to(x, (8, LANES))


def across(x, width):
    return jnp.concatenate([x] * (width // LANES), axis=1)


def eliminate_rows(work, at):
    width = work.shape[1]
    end = (at // NB + 1) * NB
    count = (end - at) // 8 - 1
    sub = lax.broadcasted_iota(jnp.int32, (8, width), 0)
    pivots = [jnp.broadcast_to(work[at + i : at + i + 1, :K], (8, K)) for i in range(8)]
    block = [[whole(pivots[i][:, at + k : at + k + 1]) for k in range(i + 1)] for i in range(8)]
    columns = None
    if count:
        columns = [
            jnp.broadcast_to(work[at + 8 : end, at + k : at + k + 1], (8 * count, LANES)).reshape(
                count, 8, LANES
            )
            for k in range(8)
        ]
    lower, scaled_rows, multipliers = [], [], []
    result = None
    for j in range(8):
        inverse = lax.rsqrt(block[j][j])
        factors = [block[i][j] * inverse if i > j else None for i in range(8)]
        for k in range(j + 1, 8):
            for i in range(k, 8):
                block[i][k] = block[i][k] - factors[i] * factors[k]
        if count:
            multiplier = columns[j] * inverse[None]
            for k in range(j + 1, 8):
                columns[k] = columns[k] - multiplier * factors[k][None]
            multipliers.append(multiplier)
        row = jnp.broadcast_to(work[at + j : at + j + 1, :], (8, width))
        for q in range(j):
            row = row - across(lower[q][j], width) * scaled_rows[q]
        row = row * across(inverse, width)
        lower.append(factors)
        scaled_rows.append(row)
        result = row if result is None else jnp.where(sub >= j, row, result)
        yield
    work[at : at + 8, :] = result
    for t in range(count):
        rows = work[at + 8 + 8 * t : at + 16 + 8 * t, :]
        for j in range(8):
            rows = rows - across(multipliers[j][t], width) * scaled_rows[j]
        work[at + 8 + 8 * t : at + 16 + 8 * t, :] = rows
        yield
    if at + 8 == end and end < K:
        group = work[end - NB : end, :]
        work[end:, :] = work[end:, :] - tn_thin(group[:, end:K], group)


def eliminate(*works):
    for at in range(0, K, 8):
        for _ in zip_longest(*[eliminate_rows(work, at) for work in works]):
            pass


def leaf_kernel(parts, out, work_z, work_h):
    share = parts.shape[1] - 2 * K // PIX
    step = K // PIX
    summed = parts[:, :share, :].reshape(PIX * share, K)
    work_h[...] = tn(summed, summed)
    for part in range(PIX):
        span = slice(step * part, step * (part + 1))
        work_z[span, :K] = parts[part, share : share + step, :]
        out[2 * K + step * part : 2 * K + step * (part + 1), :] = parts[part, share + step :, :]
    row_at = lax.broadcasted_iota(jnp.int32, (K, K), 0)
    col_at = lax.broadcasted_iota(jnp.int32, (K, K), 1)
    work_z[:, K:] = jnp.where(row_at == col_at, 1.0, 0.0)
    eliminate(work_z, work_h)
    inverse = work_z[:, K:]
    factor = nt(inverse, jnp.where(col_at >= row_at, work_h[...], 0.0))
    out[:K, :] = tn(inverse, factor)
    out[K : 2 * K, :] = tn(factor, factor)


def joined(gram, front_gram, cross, back_gram):
    largest = jnp.maximum(
        jnp.max(front_gram, keepdims=True), jnp.max(back_gram, keepdims=True)
    )
    scale = 1.0 / largest
    gram[:K, :K] = front_gram * scale
    gram[:K, K:] = cross * scale
    gram[K:, :K] = cross.T * scale
    gram[K:, K:] = back_gram * scale
    return largest, scale


def prepared(gram, work, last):
    powered = nn(gram[:K, :], gram[...])
    if last:
        work[:, :K] = nt(nn(powered, gram[...]), powered)
    else:
        work[:, :K] = nt(powered, powered)
    work[:, K:] = powered


def finish_pair(lead, core, keys, front, back, coefficients, largest, out, merged, gram, work):
    rows = front.shape[0]
    half = K // 2
    second = core[:1, :] > 0.5
    prepared(gram, work, False)
    eliminate(work)
    rotation = work[:, K:]
    if coefficients is None:
        out[:rows, :] = tall(front[...], rotation[:, :K], True) + tall(
            back[...], rotation[:, K:], True
        )
    else:
        left, right = coefficients
        out[:rows, :] = tall(front[...], nt(left, rotation[:, :K]), False) + tall(
            back[...], nt(right, rotation[:, K:]), False
        )
    fresh = nt(nn(rotation, gram[...]), rotation) * largest
    merged[...] = fresh
    out[rows : rows + half, :] = jnp.where(second, fresh[half:, :], fresh[:half, :])
    out[rows + half :, :] = jnp.minimum(keys[:8, :], keys[8:, :])


def first_kernel(core, keys, own, other, front, back, out, merged, gram, work):
    lead = keys[:1, :] < keys[8:9, :]
    left = jnp.where(lead, own[:K, :], other[:K, :])
    right = jnp.where(lead, other[:K, :], own[:K, :])
    cross = own[2 * K :, :] + other[2 * K :, :]
    largest, _ = joined(
        gram,
        jnp.where(lead, own[K : 2 * K, :], other[K : 2 * K, :]),
        nn(tn(left, cross), right),
        jnp.where(lead, other[K : 2 * K, :], own[K : 2 * K, :]),
    )
    finish_pair(lead, core, keys, front, back, (left, right), largest, out, merged, gram, work)


def merge_kernel(core, keys, mine, other, own_gram, partner_gram, front, back, *refs):
    out, merged, gram, work = refs
    second = core[:1, :] > 0.5
    lead = keys[:1, :] < keys[8:9, :]
    top = jnp.where(second, other[...], mine[...])
    low = jnp.where(second, mine[...], other[...])
    largest, _ = joined(
        gram,
        jnp.where(lead, own_gram[...], partner_gram[...]),
        jnp.concatenate([top, low], axis=0),
        jnp.where(lead, partner_gram[...], own_gram[...]),
    )
    finish_pair(lead, core, keys, front, back, None, largest, out, merged, gram, work)


PAIRS = ((0, 1), (2, 3), (0, 2), (0, 3), (1, 2), (1, 3))


def cross_kernel(panels, out):
    rows = panels.shape[1] - K // 2 - 8
    for at, (i, j) in enumerate(PAIRS):
        out[K * at : K * (at + 1), :] = tn(panels[i, :rows, :], panels[j, :rows, :])


def quad_kernel(last, core, mine, other, panels, *refs):
    out, (gram_a, gram_b, work_a, work_b) = refs[0], refs[-4:]
    half = K // 2
    shares = 3 * K
    rows = panels.shape[1] - half - 8
    second = core[:1, :] > 0.5

    def gram_of(i):
        own = panels[i, rows : rows + half, :]
        got = other[shares + half * i : shares + half * (i + 1), :]
        return jnp.concatenate(
            [jnp.where(second, got, own), jnp.where(second, own, got)], axis=0
        )

    def cross_of(pair):
        at = PAIRS.index(pair)
        share, lane = divmod(at, 3)
        span = slice(lane * K, lane * K + K)
        if share == 0:
            return jnp.where(second, other[span, :], mine[span, :])
        return jnp.where(second, mine[span, :], other[span, :])

    def key_of(i):
        return panels[i, rows + half : rows + half + 1, :]

    def ordered(lead, first_gram, cross, second_gram, gram):
        return joined(
            gram,
            jnp.where(lead, first_gram, second_gram),
            jnp.where(lead, cross, cross.T),
            jnp.where(lead, second_gram, first_gram),
        )

    def parted(lead, rotation):
        left, right = rotation[:, :K], rotation[:, K:]
        return jnp.where(lead, left, right), jnp.where(lead, right, left)

    lead_a, lead_b = key_of(0) < key_of(1), key_of(2) < key_of(3)
    largest_a, _ = ordered(lead_a, gram_of(0), cross_of((0, 1)), gram_of(1), gram_a)
    largest_b, _ = ordered(lead_b, gram_of(2), cross_of((2, 3)), gram_of(3), gram_b)
    prepared(gram_a, work_a, False)
    prepared(gram_b, work_b, False)
    eliminate(work_a, work_b)
    rotation_a, rotation_b = work_a[:, K:], work_b[:, K:]
    merged_a = nt(nn(rotation_a, gram_a[...]), rotation_a) * largest_a
    merged_b = nt(nn(rotation_b, gram_b[...]), rotation_b) * largest_b
    part_0, part_1 = parted(lead_a, rotation_a)
    part_2, part_3 = parted(lead_b, rotation_b)
    mixed_2 = nn(part_0, cross_of((0, 2))) + nn(part_1, cross_of((1, 2)))
    mixed_3 = nn(part_0, cross_of((0, 3))) + nn(part_1, cross_of((1, 3)))
    cross = nt(mixed_2, part_2) + nt(mixed_3, part_3)
    key_a = jnp.minimum(key_of(0), key_of(1))
    key_b = jnp.minimum(key_of(2), key_of(3))
    lead = key_a < key_b
    largest, scale = ordered(lead, merged_a, cross, merged_b, gram_a)
    prepared(gram_a, work_a, last)
    eliminate(work_a)
    rotation = work_a[:, K:]
    left, right = parted(lead, rotation)
    panel = tall(panels[0, :rows, :], nn(left, part_0), True)
    panel = panel + tall(panels[1, :rows, :], nn(left, part_1), True)
    panel = panel + tall(panels[2, :rows, :], nn(right, part_2), True)
    panel = panel + tall(panels[3, :rows, :], nn(right, part_3), True)
    if last:
        out[...] = panel * (math.sqrt(NPIX) * jnp.sqrt(scale))
    else:
        out[:rows, :] = panel
        fresh = nt(nn(rotation, gram_a[...]), rotation) * largest
        out[rows : rows + half, :] = jnp.where(second, fresh[half:, :], fresh[:half, :])
        out[rows + half :, :] = jnp.broadcast_to(jnp.minimum(key_a, key_b), (8, K))


def swapped(block, axis, bit):
    count = lax.axis_size(axis)
    return lax.ppermute(block, axis, [(low, low ^ 1 << bit) for low in range(count)])


def spread(block):
    many = jnp.broadcast_to(block[None], (PIX,) + block.shape)
    return lax.all_to_all(many, "pix", 0, 0)


def per_device(spectra, sketch, block_mask, rank_key):
    batch, width = spectra.shape
    share = batch // PIX
    rows = width // 2
    half = K // 2
    second = lax.axis_index("gal") % 2 == 1
    core_rows = jnp.broadcast_to(second.astype(jnp.float32), (8, K))
    pixel_mask = jnp.repeat(block_mask[0], width // block_mask.shape[1]).astype(jnp.bfloat16)
    masked = spectra * pixel_mask[None, :]
    sketched = lax.dot_general(
        masked, sketch, (((0,), (0,)), ((), ())), preferred_element_type=jnp.float32
    )
    sketch_gram = tn(sketched, sketched)
    key_rows = jnp.broadcast_to(rank_key.astype(jnp.float32)[:, None], (8, K))
    kept = jnp.where(second, sketched[rows:], sketched[:rows])
    sent = jnp.where(second, sketched[:rows], sketched[rows:])
    got = swapped(jnp.concatenate([sent, key_rows], axis=0), "gal", 0)
    high = lax.reduce_precision(sketched, 8, 7)
    low = sketched - high
    pieces = jnp.concatenate([high.astype(jnp.bfloat16), low.astype(jnp.bfloat16)], axis=1)
    both = jnp.dot(masked, pieces, preferred_element_type=jnp.float32)
    projected = both[:, :K] + both[:, K:]
    lead = key_rows[:1] < got[rows : rows + 1]
    front = jnp.where(lead, kept, got[:rows])
    back = jnp.where(lead, got[:rows], kept)
    sends = jnp.concatenate(
        [
            projected.reshape(PIX, share, K),
            sketch_gram.reshape(PIX, K // PIX, K),
            tn(front, back).reshape(PIX, K // PIX, K),
        ],
        axis=1,
    )
    parts = spread(jnp.sum(lax.all_to_all(sends, "pix", 0, 0), axis=0))
    own = pl.pallas_call(
        leaf_kernel,
        out_shape=jax.ShapeDtypeStruct((3 * K, K), jnp.float32),
        scratch_shapes=[pltpu.VMEM((K, 2 * K), jnp.float32), pltpu.VMEM((K, K), jnp.float32)],
        compiler_params=PARAMS,
        name="leaf",
    )(parts)
    pair_out = [
        jax.ShapeDtypeStruct((rows + half + 8, K), jnp.float32),
        jax.ShapeDtypeStruct((K, K), jnp.float32),
    ]
    pair_scratch = [
        pltpu.VMEM((2 * K, 2 * K), jnp.float32),
        pltpu.VMEM((K, 3 * K), jnp.float32),
    ]
    state, own_gram = pl.pallas_call(
        first_kernel,
        out_shape=pair_out,
        scratch_shapes=pair_scratch,
        compiler_params=PARAMS,
        name="first",
    )(
        core_rows,
        jnp.concatenate([key_rows, got[rows:]], axis=0),
        own,
        swapped(own, "gal", 0),
        front,
        back,
    )
    got = swapped(state, "gal", 1)
    kept, key_rows = state[:rows], state[rows + half :]
    lead = key_rows[:1] < got[rows + half : rows + half + 1]
    front = jnp.where(lead, kept, got[:rows])
    back = jnp.where(lead, got[:rows], kept)
    cross = tn(front, back)
    cross_sent = jnp.where(second, cross[:half], cross[half:])
    cross_kept = jnp.where(second, cross[half:], cross[:half])
    cross = cross_kept + swapped(cross_sent, "gal", 0)
    pair_keys = jnp.concatenate([key_rows, got[rows + half :]], axis=0)
    cross, gram_half, pair_keys = lax.optimization_barrier(
        (cross, got[rows : rows + half], pair_keys)
    )
    mine = jnp.sum(spread(cross), axis=0)
    other = swapped(jnp.concatenate([mine, gram_half], axis=0), "gal", 0)
    partner_gram = jnp.concatenate(
        [
            jnp.where(second, other[half:], gram_half),
            jnp.where(second, gram_half, other[half:]),
        ],
        axis=0,
    )
    upper = lax.axis_index("gal") // 2 % 2 == 1
    quarter = rows // 2
    front = jnp.where(upper, front[quarter:], front[:quarter])
    back = jnp.where(upper, back[quarter:], back[:quarter])
    state, own_gram = pl.pallas_call(
        merge_kernel,
        out_shape=[jax.ShapeDtypeStruct((quarter + half + 8, K), jnp.float32), pair_out[1]],
        scratch_shapes=pair_scratch,
        compiler_params=PARAMS,
        name="merge",
    )(
        core_rows,
        pair_keys,
        mine,
        other[:half],
        own_gram,
        partner_gram,
        front,
        back,
    )
    count = lax.axis_size("gal")
    both = [
        [(base + chip) * PIX + pix for chip in (0, 2) for pix in range(PIX)]
        for base in range(count)
        if not base & 2
    ]
    for level in (2, 4):
        last = level == 4
        if last:
            groups = [
                [base + (part << level) for part in range(4)]
                for base in range(count)
                if not base >> level & 3
            ]
            sends = jnp.broadcast_to(state[None], (4,) + state.shape)
            panels = lax.all_to_all(sends, "gal", 0, 0, axis_index_groups=groups)
        else:
            near = [state] + [
                lax.ppermute(state, "gal", [(at, at ^ part << level) for at in range(count)])
                for part in (1, 2, 3)
            ]
            place = lax.axis_index("gal") >> level
            odd, high = place % 2 == 1, place // 2 % 2 == 1
            near = [jnp.where(odd, near[part ^ 1], near[part]) for part in range(4)]
            panels = jnp.stack([jnp.where(high, near[part ^ 2], near[part]) for part in range(4)])
        cross = pl.pallas_call(
            cross_kernel,
            out_shape=jax.ShapeDtypeStruct((len(PAIRS) * K, K), jnp.float32),
            compiler_params=PARAMS,
            name="cross",
        )(panels)
        cross_sent = jnp.where(second, cross[: 3 * K], cross[3 * K :])
        cross_kept = jnp.where(second, cross[3 * K :], cross[: 3 * K])
        cross = cross_kept + swapped(cross_sent, "gal", 0)
        halves = panels[:, quarter : quarter + half].reshape(4 * half, K)
        cross, halves = lax.optimization_barrier((cross, halves))
        size = len(both[0])

        def exchanged(blocks):
            return lax.all_to_all(blocks, ("gal", "pix"), 0, 0, axis_index_groups=both)

        own = jnp.sum(exchanged(cross.reshape(size, -1, K)), axis=0)
        mine = exchanged(jnp.broadcast_to(own[None], (size,) + own.shape)).reshape(3 * K, K)
        other = swapped(jnp.concatenate([mine, halves], axis=0), "gal", 0)
        state = pl.pallas_call(
            functools.partial(quad_kernel, last),
            out_shape=jax.ShapeDtypeStruct((quarter + (0 if last else half + 8), K), jnp.float32),
            scratch_shapes=pair_scratch[:1] * 2 + pair_scratch[1:] * 2,
            compiler_params=PARAMS,
            name="finish" if last else "quad",
        )(core_rows, mine, other, panels)
    other = swapped(state, "gal", 1)
    state = jnp.concatenate(
        [jnp.where(upper, other, state), jnp.where(upper, state, other)], axis=0
    )
    other = swapped(state, "gal", 0)
    basis = jnp.concatenate(
        [jnp.where(second, other, state), jnp.where(second, state, other)], axis=0
    )
    score_terms = jnp.dot(masked, basis.astype(jnp.bfloat16), preferred_element_type=jnp.float32)
    own_scores = jnp.sum(
        lax.all_to_all(score_terms.reshape(PIX, share, K), "pix", 0, 0), axis=0
    )
    scores = spread(own_scores * (1.0 / NPIX)).reshape(batch, K)
    return (basis, scores)


def solution(mesh):
    in_specs = (P("gal", "pix"), P("gal", None), P("gal", "pix"), P("gal"))
    out_specs = (P("pix", None), P("gal", None))
    return jax.shard_map(
        per_device, mesh=mesh, in_specs=in_specs, out_specs=out_specs, check_vma=False
    )
```

```python
import functools
import math
from itertools import zip_longest

import jax
import jax.numpy as jnp
from jax import lax
from jax.experimental import pallas as pl
from jax.experimental.pallas import tpu as pltpu
from jax.sharding import PartitionSpec as P

NPIX = 8192
K = 128
PIX = 8
HIGH = lax.Precision.HIGHEST
PARAMS = pltpu.CompilerParams(vmem_limit_bytes=32 * 1024 * 1024)
NB = 32
LANES = 128


def dot_of(a, b, dims):
    return lax.dot_general(
        a, b, (dims, ((), ())), precision=HIGH, preferred_element_type=jnp.float32
    )


def nn(a, b):
    return dot_of(a, b, ((1,), (0,)))


def nt(a, b):
    return dot_of(a, b, ((1,), (1,)))


def tn(a, b):
    return dot_of(a, b, ((0,), (0,)))


def split2(x):
    high = x.astype(jnp.bfloat16)
    return high, (x - high.astype(jnp.float32)).astype(jnp.bfloat16)


def short(a, b, dims):
    a_high, a_low = split2(a)
    b_high, b_low = split2(b)

    def one(left, right):
        return lax.dot_general(
            left, right, (dims, ((), ())), preferred_element_type=jnp.float32
        )

    return one(a_high, b_high) + (one(a_high, b_low) + one(a_low, b_high))


def short_nn(a, b):
    return short(a, b, ((1,), (0,)))


def short_nt(a, b):
    return short(a, b, ((1,), (1,)))


def tall(panel, factor, turned):
    return short_nt(panel, factor) if turned else short_nn(panel, factor)


def split3(x):
    high = x.astype(jnp.bfloat16)
    rest = x - high.astype(jnp.float32)
    middle = rest.astype(jnp.bfloat16)
    low = (rest - middle.astype(jnp.float32)).astype(jnp.bfloat16)
    return high, middle, low


def tn_thin(a, b):
    ah, am, al = split3(a)
    bh, bm, bl = split3(b)
    left = jnp.concatenate([ah, ah, am, am, ah, al], axis=0)
    right = jnp.concatenate([bh, bm, bh, bm, bl, bh], axis=0)
    return lax.dot_general(
        left, right, (((0,), (0,)), ((), ())), preferred_element_type=jnp.float32
    )


def whole(x):
    return jnp.broadcast_to(x, (8, LANES))


def across(x, width):
    return jnp.concatenate([x] * (width // LANES), axis=1)


def eliminate_rows(work, at):
    width = work.shape[1]
    end = (at // NB + 1) * NB
    count = (end - at) // 8 - 1
    sub = lax.broadcasted_iota(jnp.int32, (8, width), 0)
    pivots = [jnp.broadcast_to(work[at + i : at + i + 1, :K], (8, K)) for i in range(8)]
    block = [[whole(pivots[i][:, at + k : at + k + 1]) for k in range(i + 1)] for i in range(8)]
    columns = None
    if count:
        columns = [
            jnp.broadcast_to(work[at + 8 : end, at + k : at + k + 1], (8 * count, LANES)).reshape(
                count, 8, LANES
            )
            for k in range(8)
        ]
    lower, scaled_rows, multipliers = [], [], []
    result = None
    for j in range(8):
        inverse = lax.rsqrt(block[j][j])
        factors = [block[i][j] * inverse if i > j else None for i in range(8)]
        for k in range(j + 1, 8):
            for i in range(k, 8):
                block[i][k] = block[i][k] - factors[i] * factors[k]
        if count:
            multiplier = columns[j] * inverse[None]
            for k in range(j + 1, 8):
                columns[k] = columns[k] - multiplier * factors[k][None]
            multipliers.append(multiplier)
        row = jnp.broadcast_to(work[at + j : at + j + 1, :], (8, width))
        for q in range(j):
            row = row - across(lower[q][j], width) * scaled_rows[q]
        row = row * across(inverse, width)
        lower.append(factors)
        scaled_rows.append(row)
        result = row if result is None else jnp.where(sub >= j, row, result)
        yield
    work[at : at + 8, :] = result
    for t in range(count):
        rows = work[at + 8 + 8 * t : at + 16 + 8 * t, :]
        for j in range(8):
            rows = rows - across(multipliers[j][t], width) * scaled_rows[j]
        work[at + 8 + 8 * t : at + 16 + 8 * t, :] = rows
        yield
    if at + 8 == end and end < K:
        group = work[end - NB : end, :]
        work[end:, :] = work[end:, :] - tn_thin(group[:, end:K], group)


def eliminate(*works):
    for at in range(0, K, 8):
        for _ in zip_longest(*[eliminate_rows(work, at) for work in works]):
            pass


def leaf_kernel(parts, out, work_z, work_h):
    share = parts.shape[1] - 2 * K // PIX
    step = K // PIX
    summed = parts[:, :share, :].reshape(PIX * share, K)
    work_h[...] = tn(summed, summed)
    for part in range(PIX):
        span = slice(step * part, step * (part + 1))
        work_z[span, :K] = parts[part, share : share + step, :]
        out[2 * K + step * part : 2 * K + step * (part + 1), :] = parts[part, share + step :, :]
    row_at = lax.broadcasted_iota(jnp.int32, (K, K), 0)
    col_at = lax.broadcasted_iota(jnp.int32, (K, K), 1)
    work_z[:, K:] = jnp.where(row_at == col_at, 1.0, 0.0)
    eliminate(work_z, work_h)
    inverse = work_z[:, K:]
    factor = nt(inverse, jnp.where(col_at >= row_at, work_h[...], 0.0))
    out[:K, :] = tn(inverse, factor)
    out[K : 2 * K, :] = tn(factor, factor)


def joined(gram, front_gram, cross, back_gram):
    largest = jnp.maximum(
        jnp.max(front_gram, keepdims=True), jnp.max(back_gram, keepdims=True)
    )
    scale = 1.0 / largest
    gram[:K, :K] = front_gram * scale
    gram[:K, K:] = cross * scale
    gram[K:, :K] = cross.T * scale
    gram[K:, K:] = back_gram * scale
    return largest, scale


def prepared(gram, work, last):
    powered = nn(gram[:K, :], gram[...])
    if last:
        work[:, :K] = nt(nn(powered, gram[...]), powered)
    else:
        work[:, :K] = nt(powered, powered)
    work[:, K:] = powered


def finish_pair(lead, core, keys, front, back, coefficients, largest, out, merged, gram, work):
    rows = front.shape[0]
    half = K // 2
    second = core[:1, :] > 0.5
    prepared(gram, work, False)
    eliminate(work)
    rotation = work[:, K:]
    if coefficients is None:
        out[:rows, :] = tall(front[...], rotation[:, :K], True) + tall(
            back[...], rotation[:, K:], True
        )
    else:
        left, right = coefficients
        out[:rows, :] = tall(front[...], short_nt(left, rotation[:, :K]), False) + tall(
            back[...], short_nt(right, rotation[:, K:]), False
        )
    fresh = short_nt(short_nn(rotation, gram[...]), rotation) * largest
    merged[...] = fresh
    out[rows : rows + half, :] = jnp.where(second, fresh[half:, :], fresh[:half, :])
    out[rows + half :, :] = jnp.minimum(keys[:8, :], keys[8:, :])


def first_kernel(core, keys, own, other, front, back, out, merged, gram, work):
    lead = keys[:1, :] < keys[8:9, :]
    left = jnp.where(lead, own[:K, :], other[:K, :])
    right = jnp.where(lead, other[:K, :], own[:K, :])
    cross = own[2 * K :, :] + other[2 * K :, :]
    largest, _ = joined(
        gram,
        jnp.where(lead, own[K : 2 * K, :], other[K : 2 * K, :]),
        nn(tn(left, cross), right),
        jnp.where(lead, other[K : 2 * K, :], own[K : 2 * K, :]),
    )
    finish_pair(lead, core, keys, front, back, (left, right), largest, out, merged, gram, work)


def merge_kernel(core, keys, mine, other, own_gram, partner_gram, front, back, *refs):
    out, merged, gram, work = refs
    second = core[:1, :] > 0.5
    lead = keys[:1, :] < keys[8:9, :]
    top = jnp.where(second, other[...], mine[...])
    low = jnp.where(second, mine[...], other[...])
    largest, _ = joined(
        gram,
        jnp.where(lead, own_gram[...], partner_gram[...]),
        jnp.concatenate([top, low], axis=0),
        jnp.where(lead, partner_gram[...], own_gram[...]),
    )
    finish_pair(lead, core, keys, front, back, None, largest, out, merged, gram, work)


PAIRS = ((0, 1), (2, 3), (0, 2), (0, 3), (1, 2), (1, 3))


def cross_kernel(panels, out):
    rows = panels.shape[1] - K // 2 - 8
    for at, (i, j) in enumerate(PAIRS):
        out[K * at : K * (at + 1), :] = tn(panels[i, :rows, :], panels[j, :rows, :])


def quad_kernel(last, core, mine, other, panels, *refs):
    out, (gram_a, gram_b, work_a, work_b) = refs[0], refs[-4:]
    half = K // 2
    shares = 3 * K
    rows = panels.shape[1] - half - 8
    second = core[:1, :] > 0.5

    def gram_of(i):
        own = panels[i, rows : rows + half, :]
        got = other[shares + half * i : shares + half * (i + 1), :]
        return jnp.concatenate(
            [jnp.where(second, got, own), jnp.where(second, own, got)], axis=0
        )

    def cross_of(pair):
        at = PAIRS.index(pair)
        share, lane = divmod(at, 3)
        span = slice(lane * K, lane * K + K)
        if share == 0:
            return jnp.where(second, other[span, :], mine[span, :])
        return jnp.where(second, mine[span, :], other[span, :])

    def key_of(i):
        return panels[i, rows + half : rows + half + 1, :]

    def ordered(lead, first_gram, cross, second_gram, gram):
        return joined(
            gram,
            jnp.where(lead, first_gram, second_gram),
            jnp.where(lead, cross, cross.T),
            jnp.where(lead, second_gram, first_gram),
        )

    def parted(lead, rotation):
        left, right = rotation[:, :K], rotation[:, K:]
        return jnp.where(lead, left, right), jnp.where(lead, right, left)

    lead_a, lead_b = key_of(0) < key_of(1), key_of(2) < key_of(3)
    largest_a, _ = ordered(lead_a, gram_of(0), cross_of((0, 1)), gram_of(1), gram_a)
    largest_b, _ = ordered(lead_b, gram_of(2), cross_of((2, 3)), gram_of(3), gram_b)
    prepared(gram_a, work_a, False)
    prepared(gram_b, work_b, False)
    eliminate(work_a, work_b)
    rotation_a, rotation_b = work_a[:, K:], work_b[:, K:]
    merged_a = short_nt(short_nn(rotation_a, gram_a[...]), rotation_a) * largest_a
    merged_b = short_nt(short_nn(rotation_b, gram_b[...]), rotation_b) * largest_b
    part_0, part_1 = parted(lead_a, rotation_a)
    part_2, part_3 = parted(lead_b, rotation_b)
    mixed_2 = short_nn(part_0, cross_of((0, 2))) + short_nn(part_1, cross_of((1, 2)))
    mixed_3 = short_nn(part_0, cross_of((0, 3))) + short_nn(part_1, cross_of((1, 3)))
    cross = short_nt(mixed_2, part_2) + short_nt(mixed_3, part_3)
    key_a = jnp.minimum(key_of(0), key_of(1))
    key_b = jnp.minimum(key_of(2), key_of(3))
    lead = key_a < key_b
    largest, scale = ordered(lead, merged_a, cross, merged_b, gram_a)
    prepared(gram_a, work_a, last)
    eliminate(work_a)
    rotation = work_a[:, K:]
    left, right = parted(lead, rotation)
    panel = tall(panels[0, :rows, :], short_nn(left, part_0), True)
    panel = panel + tall(panels[1, :rows, :], short_nn(left, part_1), True)
    panel = panel + tall(panels[2, :rows, :], short_nn(right, part_2), True)
    panel = panel + tall(panels[3, :rows, :], short_nn(right, part_3), True)
    if last:
        out[...] = panel * (math.sqrt(NPIX) * jnp.sqrt(scale))
    else:
        out[:rows, :] = panel
        fresh = short_nt(short_nn(rotation, gram_a[...]), rotation) * largest
        out[rows : rows + half, :] = jnp.where(second, fresh[half:, :], fresh[:half, :])
        out[rows + half :, :] = jnp.broadcast_to(jnp.minimum(key_a, key_b), (8, K))


def swapped(block, axis, bit):
    count = lax.axis_size(axis)
    return lax.ppermute(block, axis, [(low, low ^ 1 << bit) for low in range(count)])


def spread(block):
    many = jnp.broadcast_to(block[None], (PIX,) + block.shape)
    return lax.all_to_all(many, "pix", 0, 0)


def per_device(spectra, sketch, block_mask, rank_key):
    batch, width = spectra.shape
    share = batch // PIX
    rows = width // 2
    half = K // 2
    second = lax.axis_index("gal") % 2 == 1
    core_rows = jnp.broadcast_to(second.astype(jnp.float32), (8, K))
    pixel_mask = jnp.repeat(block_mask[0], width // block_mask.shape[1]).astype(jnp.bfloat16)
    masked = spectra * pixel_mask[None, :]
    sketched = lax.dot_general(
        masked, sketch, (((0,), (0,)), ((), ())), preferred_element_type=jnp.float32
    )
    sketch_gram = tn(sketched, sketched)
    key_rows = jnp.broadcast_to(rank_key.astype(jnp.float32)[:, None], (8, K))
    kept = jnp.where(second, sketched[rows:], sketched[:rows])
    sent = jnp.where(second, sketched[:rows], sketched[rows:])
    got = swapped(jnp.concatenate([sent, key_rows], axis=0), "gal", 0)
    high = lax.reduce_precision(sketched, 8, 7)
    low = sketched - high
    pieces = jnp.concatenate([high.astype(jnp.bfloat16), low.astype(jnp.bfloat16)], axis=1)
    both = jnp.dot(masked, pieces, preferred_element_type=jnp.float32)
    projected = both[:, :K] + both[:, K:]
    lead = key_rows[:1] < got[rows : rows + 1]
    front = jnp.where(lead, kept, got[:rows])
    back = jnp.where(lead, got[:rows], kept)
    sends = jnp.concatenate(
        [
            projected.reshape(PIX, share, K),
            sketch_gram.reshape(PIX, K // PIX, K),
            tn(front, back).reshape(PIX, K // PIX, K),
        ],
        axis=1,
    )
    parts = spread(jnp.sum(lax.all_to_all(sends, "pix", 0, 0), axis=0))
    own = pl.pallas_call(
        leaf_kernel,
        out_shape=jax.ShapeDtypeStruct((3 * K, K), jnp.float32),
        scratch_shapes=[pltpu.VMEM((K, 2 * K), jnp.float32), pltpu.VMEM((K, K), jnp.float32)],
        compiler_params=PARAMS,
        name="leaf",
    )(parts)
    pair_out = [
        jax.ShapeDtypeStruct((rows + half + 8, K), jnp.float32),
        jax.ShapeDtypeStruct((K, K), jnp.float32),
    ]
    pair_scratch = [
        pltpu.VMEM((2 * K, 2 * K), jnp.float32),
        pltpu.VMEM((K, 3 * K), jnp.float32),
    ]
    state, own_gram = pl.pallas_call(
        first_kernel,
        out_shape=pair_out,
        scratch_shapes=pair_scratch,
        compiler_params=PARAMS,
        name="first",
    )(
        core_rows,
        jnp.concatenate([key_rows, got[rows:]], axis=0),
        own,
        swapped(own, "gal", 0),
        front,
        back,
    )
    got = swapped(state, "gal", 1)
    kept, key_rows = state[:rows], state[rows + half :]
    lead = key_rows[:1] < got[rows + half : rows + half + 1]
    front = jnp.where(lead, kept, got[:rows])
    back = jnp.where(lead, got[:rows], kept)
    cross = tn(front, back)
    cross_sent = jnp.where(second, cross[:half], cross[half:])
    cross_kept = jnp.where(second, cross[half:], cross[:half])
    cross = cross_kept + swapped(cross_sent, "gal", 0)
    pair_keys = jnp.concatenate([key_rows, got[rows + half :]], axis=0)
    upper = lax.axis_index("gal") // 2 % 2 == 1
    quarter = rows // 2
    front = jnp.where(upper, front[quarter:], front[:quarter])
    back = jnp.where(upper, back[quarter:], back[:quarter])
    cross, gram_half, pair_keys, front, back = lax.optimization_barrier(
        (cross, got[rows : rows + half], pair_keys, front, back)
    )
    mine = jnp.sum(spread(cross), axis=0)
    other = swapped(jnp.concatenate([mine, gram_half], axis=0), "gal", 0)
    partner_gram = jnp.concatenate(
        [
            jnp.where(second, other[half:], gram_half),
            jnp.where(second, gram_half, other[half:]),
        ],
        axis=0,
    )
    state, own_gram = pl.pallas_call(
        merge_kernel,
        out_shape=[jax.ShapeDtypeStruct((quarter + half + 8, K), jnp.float32), pair_out[1]],
        scratch_shapes=pair_scratch,
        compiler_params=PARAMS,
        name="merge",
    )(
        core_rows,
        pair_keys,
        mine,
        other[:half],
        own_gram,
        partner_gram,
        front,
        back,
    )
    count = lax.axis_size("gal")
    both = [
        [(base + chip) * PIX + pix for chip in (0, 2) for pix in range(PIX)]
        for base in range(count)
        if not base & 2
    ]
    for level in (2, 4):
        last = level == 4
        if last:
            groups = [
                [base + (part << level) for part in range(4)]
                for base in range(count)
                if not base >> level & 3
            ]
            sends = jnp.broadcast_to(state[None], (4,) + state.shape)
            panels = lax.all_to_all(sends, "gal", 0, 0, axis_index_groups=groups)
        else:
            near = [state] + [
                lax.ppermute(state, "gal", [(at, at ^ part << level) for at in range(count)])
                for part in (1, 2, 3)
            ]
            place = lax.axis_index("gal") >> level
            odd, high = place % 2 == 1, place // 2 % 2 == 1
            near = [jnp.where(odd, near[part ^ 1], near[part]) for part in range(4)]
            panels = jnp.stack([jnp.where(high, near[part ^ 2], near[part]) for part in range(4)])
        cross = pl.pallas_call(
            cross_kernel,
            out_shape=jax.ShapeDtypeStruct((len(PAIRS) * K, K), jnp.float32),
            compiler_params=PARAMS,
            name="cross",
        )(panels)
        cross_sent = jnp.where(second, cross[: 3 * K], cross[3 * K :])
        cross_kept = jnp.where(second, cross[3 * K :], cross[: 3 * K])
        cross = cross_kept + swapped(cross_sent, "gal", 0)
        halves = panels[:, quarter : quarter + half].reshape(4 * half, K)
        cross, halves = lax.optimization_barrier((cross, halves))
        size = len(both[0])

        def exchanged(blocks):
            return lax.all_to_all(blocks, ("gal", "pix"), 0, 0, axis_index_groups=both)

        own = jnp.sum(exchanged(cross.reshape(size, -1, K)), axis=0)
        mine = exchanged(jnp.broadcast_to(own[None], (size,) + own.shape)).reshape(3 * K, K)
        other = swapped(jnp.concatenate([mine, halves], axis=0), "gal", 0)
        state = pl.pallas_call(
            functools.partial(quad_kernel, last),
            out_shape=jax.ShapeDtypeStruct((quarter + (0 if last else half + 8), K), jnp.float32),
            scratch_shapes=pair_scratch[:1] * 2 + pair_scratch[1:] * 2,
            compiler_params=PARAMS,
            name="finish" if last else "quad",
        )(core_rows, mine, other, panels)
    other = swapped(state, "gal", 1)
    state = jnp.concatenate(
        [jnp.where(upper, other, state), jnp.where(upper, state, other)], axis=0
    )
    other = swapped(state, "gal", 0)
    basis = jnp.concatenate(
        [jnp.where(second, other, state), jnp.where(second, state, other)], axis=0
    )
    score_terms = jnp.dot(masked, basis.astype(jnp.bfloat16), preferred_element_type=jnp.float32)
    own_scores = jnp.sum(
        lax.all_to_all(score_terms.reshape(PIX, share, K), "pix", 0, 0), axis=0
    )
    scores = spread(own_scores * (1.0 / NPIX)).reshape(batch, K)
    return (basis, scores)


def solution(mesh):
    in_specs = (P("gal", "pix"), P("gal", None), P("gal", "pix"), P("gal"))
    out_specs = (P("pix", None), P("gal", None))
    return jax.shard_map(
        per_device, mesh=mesh, in_specs=in_specs, out_specs=out_specs, check_vma=False
    )
```
